256 devices in a mesh: path: 32 (over z, x), fsdp: 8 (over y, core).
Axes of the slice: x: 4, y: 4, z: 8, core: 2. Of those that a mesh axis runs over, the one named last changes fastest.
Arguments:
- hidden_in: bfloat16 [32, 1024, 1024], P('path', 'fsdp'), may hold values from -40 to 40
- cotangent: bfloat16 [32, 1024, 1024], P('path', 'fsdp'), may hold values from -6 to 6
- up_weight: bfloat16 [32, 1024, 4096], P(None, 'path', 'fsdp'), may hold values from -4 to 4
- down_weight: bfloat16 [32, 1024, 4096], P(None, 'path', 'fsdp'), may hold values from -4 to 4
- up_moment: bfloat16 [32, 1024, 4096], P(None, 'path', 'fsdp'), may hold values from -3 to 3
- down_moment: bfloat16 [32, 1024, 4096], P(None, 'path', 'fsdp'), may hold values from -3 to 3
- sharing: int32 [32, 2], replicated, may hold values from 0 to 31, as said below
Outputs:
- new_up: bfloat16 [32, 1024, 4096], P(None, 'path', 'fsdp')
- new_down: bfloat16 [32, 1024, 4096], P(None, 'path', 'fsdp')
- new_up_moment: bfloat16 [32, 1024, 4096], P(None, 'path', 'fsdp')
- new_down_moment: bfloat16 [32, 1024, 4096], P(None, 'path', 'fsdp')
The draws below stay inside these ranges and needn't reach their ends.
Inputs may be any that keep to these rules, and one draw needn't show every extreme that they name: `sharing`: column 0 names a first-level module, 0 to 15; column 1 a second-level module, 16 to 31. Every module is named by at least one path.
All inputs are finite; a program needn't handle non-finite values.
Results may differ from the reference program's by a relative error of at most 0.014.
Values may be sent and summed in bfloat16 or wider, within the bound.
No kernel may reach another device: no remote copies, remote signals or barrier semaphores. Data moves between devices by JAX's collectives and lax.ppermute only.
A program may use at most 128 MiB of HBM per device.

```python
import math
import jax
import jax.numpy as jnp
from jax import lax

D = 1024
HID = 4096
PATHS = 32
MODS = 16
NMOD = 32
PATH_TOK = 1024


def draw_hidden_in(key, part):
    key = jax.random.fold_in(key, 11)
    key_base, key_rows, key_cols = jax.random.split(key, 3)
    base = jax.random.truncated_normal(key_base, -4.0, 4.0, (PATHS, PATH_TOK, D), jnp.float32)
    spread = 1.15
    row_factor = jnp.exp(jax.random.uniform(key_rows, (PATHS, PATH_TOK, 1), jnp.float32, -spread, spread))
    col_factor = jnp.exp(jax.random.uniform(key_cols, (1, 1, D), jnp.float32, -spread, spread))
    return (base * row_factor * col_factor).astype(jnp.bfloat16)


def level_column(key, level):
    key = jax.random.fold_in(key, level)
    key_one, key_two, key_three, key_label, key_order = jax.random.split(key, 5)
    extra = jnp.minimum(jax.random.randint(key_one, (PATHS - MODS,), 0, MODS), jax.random.randint(key_two, (PATHS - MODS,), 0, MODS))
    extra = jnp.minimum(extra, jax.random.randint(key_three, (PATHS - MODS,), 0, MODS))
    labels = jnp.concatenate([jnp.arange(MODS, dtype=jnp.int32), extra.astype(jnp.int32)])
    relabel = jax.random.permutation(key_label, MODS).astype(jnp.int32)
    order = jax.random.permutation(key_order, PATHS)
    return relabel[labels][order] + level * MODS


def draw_sharing(key, part):
    key = jax.random.fold_in(key, 7)
    return jnp.stack([level_column(key, 0), level_column(key, 1)], axis=1).astype(jnp.int32)


def block_levels(rng, extent, cuts, smallest, largest):
    level = 1.0
    for axis_at, parts in cuts:
        steps = jax.random.uniform(jax.random.fold_in(jax.random.fold_in(rng, 6), axis_at), (parts,), jnp.float32, smallest / len(cuts), largest / len(cuts))
        level = level * jnp.repeat(jnp.exp(steps), extent[axis_at] // parts).reshape((-1,) + (1,) * (len(extent) - 1 - axis_at))
    return level


def noise(stream_key, extent, width, most, pieces=(), kind=jnp.bfloat16):
    result = width * jax.random.normal(stream_key, extent, jnp.float32)
    if pieces:
        result = result * block_levels(stream_key, extent, pieces, -0.22, 0.18)
    return jnp.clip(result, -most, most).astype(kind)


def setup_inputs(seed: int = 0) -> dict:
    key_of = jax.random.split(jax.random.key(seed), 8)
    hidden_in = draw_hidden_in(jax.random.fold_in(key_of[7], 71), 0)
    cotangent = noise(key_of[1], (PATHS, PATH_TOK, D), 1.0, 6.0, ((0, 32), (1, 8)))
    up_weight = noise(key_of[2], (NMOD, D, HID), 1.0, 4.0, ((1, 32), (2, 8)))
    down_weight = noise(key_of[3], (NMOD, D, HID), 1.0, 4.0, ((1, 32), (2, 8)))
    up_moment = noise(key_of[4], (NMOD, D, HID), 0.5, 3.0, ((1, 32), (2, 8)))
    down_moment = noise(key_of[5], (NMOD, D, HID), 0.5, 3.0, ((1, 32), (2, 8)))
    sharing = draw_sharing(jax.random.fold_in(key_of[7], 71), 0)
    return {"hidden_in": hidden_in, "cotangent": cotangent, "up_weight": up_weight, "down_weight": down_weight, "up_moment": up_moment, "down_moment": down_moment, "sharing": sharing}


inner_rate = 2.0
outer_rate = 0.7
keep_rate = 0.9
norm_eps = 1e-06
tanh_coeff = 0.7978845608028654
cube_coeff = 0.044715

def gelu_value(values):
    inside = tanh_coeff * (values + cube_coeff * values * values * values)
    return 0.5 * values * (1.0 + jnp.tanh(inside))

def gelu_slope(values):
    inside = tanh_coeff * (values + cube_coeff * values * values * values)
    tangent = jnp.tanh(inside)
    return 0.5 * (1.0 + tangent) + 0.5 * values * (1.0 - tangent * tangent) * tanh_coeff * (1.0 + 3.0 * cube_coeff * values * values)

def row_scale(values):
    return lax.rsqrt(lax.optimization_barrier(jnp.mean(values * values, axis=-1, keepdims=True)) + norm_eps)

def path_deltas(tokens_in, cot_in, up_first, down_first, up_second, down_second):
    in_scale = 1.0 / math.sqrt(up_first.shape[0])
    hid_scale = 1.0 / math.sqrt(up_first.shape[1])
    start_vals = tokens_in.astype(jnp.float32)
    normed_first = (start_vals * row_scale(start_vals)).astype(jnp.bfloat16)
    pre_first = jnp.dot(normed_first, up_first, preferred_element_type=jnp.float32) * in_scale
    hidden_first = gelu_value(pre_first).astype(jnp.bfloat16)
    middle = start_vals + jnp.dot(hidden_first, down_first.T, preferred_element_type=jnp.float32) * hid_scale
    scale_second = row_scale(middle)
    unit_second = middle * scale_second
    normed_second = unit_second.astype(jnp.bfloat16)
    pre_second = jnp.dot(normed_second, up_second, preferred_element_type=jnp.float32) * in_scale
    hidden_second = gelu_value(pre_second).astype(jnp.bfloat16)
    back_hidden = jnp.dot(cot_in, down_second, preferred_element_type=jnp.float32) * hid_scale
    grad_down_second = jnp.dot(cot_in.T, hidden_second, preferred_element_type=jnp.float32) * hid_scale
    back_pre = (back_hidden * gelu_slope(pre_second)).astype(jnp.bfloat16)
    grad_up_second = jnp.dot(normed_second.T, back_pre, preferred_element_type=jnp.float32) * in_scale
    back_normed = jnp.dot(back_pre, up_second.T, preferred_element_type=jnp.float32) * in_scale
    back_middle = (cot_in.astype(jnp.float32) + scale_second * (back_normed - unit_second * lax.optimization_barrier(jnp.mean(back_normed * unit_second, axis=-1, keepdims=True)))).astype(jnp.bfloat16)
    back_hidden_first = jnp.dot(back_middle, down_first, preferred_element_type=jnp.float32) * hid_scale
    grad_down_first = jnp.dot(back_middle.T, hidden_first, preferred_element_type=jnp.float32) * hid_scale
    back_pre_first = (back_hidden_first * gelu_slope(pre_first)).astype(jnp.bfloat16)
    grad_up_first = jnp.dot(normed_first.T, back_pre_first, preferred_element_type=jnp.float32) * in_scale
    delta_up = (inner_rate * jnp.stack([grad_up_first, grad_up_second])).astype(jnp.bfloat16)
    delta_down = (inner_rate * jnp.stack([grad_down_first, grad_down_second])).astype(jnp.bfloat16)
    return (delta_up, delta_down)

def outer_step(weight, moment, mean_delta):
    new_moment = keep_rate * moment.astype(jnp.float32) + mean_delta
    new_weight = weight.astype(jnp.float32) - outer_rate * (mean_delta + keep_rate * new_moment)
    return (new_weight.astype(jnp.bfloat16), new_moment.astype(jnp.bfloat16))

def reference(hidden_in, cotangent, up_weight, down_weight, up_moment, down_moment, sharing):
    module_count = up_weight.shape[0]

    def one_path(totals, inputs):
        tokens_in, cot_in, pair = inputs
        first = pair[0].astype(jnp.int32)
        second = pair[1].astype(jnp.int32)
        up_first = lax.dynamic_index_in_dim(up_weight, first, 0, keepdims=False)
        down_first = lax.dynamic_index_in_dim(down_weight, first, 0, keepdims=False)
        up_second = lax.dynamic_index_in_dim(up_weight, second, 0, keepdims=False)
        down_second = lax.dynamic_index_in_dim(down_weight, second, 0, keepdims=False)
        delta_up, delta_down = path_deltas(tokens_in, cot_in, up_first, down_first, up_second, down_second)
        total_up, total_down = totals
        total_up = total_up.at[first].add(delta_up[0].astype(jnp.float32)).at[second].add(delta_up[1].astype(jnp.float32))
        total_down = total_down.at[first].add(delta_down[0].astype(jnp.float32)).at[second].add(delta_down[1].astype(jnp.float32))
        return ((total_up, total_down), None)
    zeros = jnp.zeros(up_weight.shape, jnp.float32)
    totals, unused_out = lax.scan(one_path, (zeros, zeros), (hidden_in, cotangent, sharing))
    total_up, total_down = totals
    hits = (sharing[:, :, None] == jnp.arange(module_count, dtype=jnp.int32)[None, None, :]).astype(jnp.float32)
    counts = lax.optimization_barrier(jnp.sum(hits, axis=(0, 1)))
    mean_up = total_up / counts[:, None, None]
    mean_down = total_down / counts[:, None, None]
    new_up, new_up_moment = outer_step(up_weight, up_moment, mean_up)
    new_down, new_down_moment = outer_step(down_weight, down_moment, mean_down)
    return (new_up, new_down, new_up_moment, new_down_moment)
```

```python
import functools
import math

import jax
import jax.numpy as jnp
from jax import lax
from jax.experimental import pallas as pl
from jax.experimental.pallas import tpu as pltpu
from jax.sharding import PartitionSpec as P

inner_rate = 2.0
outer_rate = 0.7
keep_rate = 0.9
norm_eps = 1e-06
tanh_coeff = 0.7978845608028654
cube_coeff = 0.044715

f32 = jnp.float32
bf16 = jnp.bfloat16
ANY = pl.BlockSpec(memory_space=pl.ANY)
SMEM = pl.BlockSpec(memory_space=pltpu.SMEM)
VMEM = pl.BlockSpec(memory_space=pltpu.VMEM)
CORES = 2


def gelu_both(values):
    square = values * values
    tangent = jnp.tanh(tanh_coeff * (values + cube_coeff * values * square))
    half = 0.5 * (1.0 + tangent)
    slope = half + 0.5 * values * (1.0 - tangent * tangent) * tanh_coeff * (
        1.0 + 3.0 * cube_coeff * square
    )
    return (values * half, slope)


def row_scale(values):
    return lax.rsqrt(jnp.mean(values * values, axis=-1, keepdims=True) + norm_eps)


def nn(left, right):
    return jnp.dot(left, right, preferred_element_type=f32)


def nt(left, right):
    return lax.dot_general(left, right, (((1,), (1,)), ((), ())), preferred_element_type=f32)


def tn(left, right):
    return lax.dot_general(left, right, (((0,), (0,)), ((), ())), preferred_element_type=f32)


def params(mib):
    return pltpu.CompilerParams(vmem_limit_bytes=mib * 1024 * 1024)


def cost(flops, moved):
    return pl.CostEstimate(flops=flops, bytes_accessed=moved, transcendentals=0)


class Copies:
    def __init__(self, sems):
        self.sems, self.used = sems, 0

    def start(self, source, target):
        copy = pltpu.make_async_copy(source, target, self.sems.at[self.used])
        self.used += 1
        copy.start()
        return copy


def pick_kernel(level, share, up_w, down_w, out, sems):
    paths = out.shape[0]
    copies = Copies(sems)
    started = []
    for p in range(paths):
        module = share[p, level]
        started.append(copies.start(up_w.at[module], out.at[p, 0]))
        started.append(copies.start(down_w.at[module], out.at[p, 1]))
    for copy in started:
        copy.wait()


def pick(sharing, up_w, down_w, level):
    paths = sharing.shape[0]
    rows, cols = up_w.shape[1:]
    return pl.pallas_call(
        functools.partial(pick_kernel, level),
        out_shape=jax.ShapeDtypeStruct((paths, 2, rows, cols), bf16),
        in_specs=[SMEM, ANY, ANY],
        out_specs=ANY,
        scratch_shapes=[pltpu.SemaphoreType.DMA((2 * paths,))],
        compiler_params=params(2),
        cost_estimate=cost(0, 4 * paths * rows * cols * 2),
        name=f"pick_{level}",
    )(sharing, up_w, down_w)


def first_kernel(scales, *refs):
    in_scale, hid_scale = scales
    n = 8
    normed, came = refs[:n], refs[n]
    own, send, hidden, slope = refs[n + 1 : n + 5]
    nbuf, ubuf, wbuf, obuf, sbuf, hbuf, dbuf, sems = refs[n + 5 :]
    copies = Copies(sems)
    get_u = copies.start(came.at[:, 0], ubuf)
    get_n = [copies.start(normed[i], nbuf.at[i // 2, pl.ds((i % 2) * 128, 128)]) for i in range(n)]
    get_w = copies.start(came.at[:, 1], wbuf)
    get_u.wait()
    put = []
    for k in range(4):
        get_n[2 * k].wait()
        get_n[2 * k + 1].wait()
        value, back = gelu_both(nn(nbuf[k], ubuf[...].reshape(1024, 512)) * in_scale)
        hbuf[k] = value.astype(bf16)
        dbuf[k] = back
        put.append(copies.start(hbuf.at[k], hidden.at[k]))
        put.append(copies.start(dbuf.at[k], slope.at[k]))
        if k == 0:
            get_w.wait()
        branch = nt(hbuf[k], wbuf[...].reshape(1024, 512)) * hid_scale
        obuf[k] = branch[:128]
        sbuf[k] = branch[128:].astype(bf16)
        put.append(copies.start(obuf.at[k], own.at[k]))
        put.append(copies.start(sbuf.at[k], send.at[k]))
    for copy in put:
        copy.wait()


def first_forward(normed, came, scales):
    shapes = [((4, 128, 1024), f32), ((4, 128, 1024), bf16), ((4, 256, 512), bf16), ((4, 256, 512), f32)]
    return pl.pallas_call(
        functools.partial(first_kernel, scales),
        out_shape=[jax.ShapeDtypeStruct(*s) for s in shapes],
        in_specs=[ANY] * 9,
        out_specs=[ANY] * 4,
        scratch_shapes=[
            pltpu.VMEM((4, 256, 1024), bf16),
            pltpu.VMEM((32, 32, 512), bf16),
            pltpu.VMEM((32, 32, 512), bf16),
        ]
        + [pltpu.VMEM(*s) for s in shapes]
        + [pltpu.SemaphoreType.DMA((26,))],
        compiler_params=params(14),
        cost_estimate=cost(2 * 2 * 1024 * 1024 * 512, 10 << 20),
        name="first_forward",
    )(*normed, came)


def second_kernel(scales, *refs):
    in_scale, hid_scale = scales
    n = 8
    normed, cots, came = refs[:n], refs[n : 2 * n], refs[2 * n]
    own, send, grads = refs[2 * n + 1 : 2 * n + 4]
    nbuf, gbuf, ubuf, wbuf, obuf, sbuf, hbuf, pbuf, outbuf, sems = refs[2 * n + 4 :]
    copies = Copies(sems)
    get_u = copies.start(came.at[:, 0], ubuf)
    get_n = [copies.start(normed[i], nbuf.at[pl.ds(i * 128, 128)]) for i in range(2)]
    get_w = copies.start(came.at[:, 1], wbuf)
    get_g = [copies.start(cots[i], gbuf.at[pl.ds(i * 128, 128)]) for i in range(2)]
    for i in range(2, n):
        get_n.append(copies.start(normed[i], nbuf.at[pl.ds(i * 128, 128)]))
        get_g.append(copies.start(cots[i], gbuf.at[pl.ds(i * 128, 128)]))
    get_u.wait()
    put = []
    for k in range(4):
        rows = pl.ds(k * 256, 256)
        get_n[2 * k].wait()
        get_n[2 * k + 1].wait()
        value, slope = gelu_both(nn(nbuf[rows], ubuf[...].reshape(1024, 512)) * in_scale)
        hbuf[rows] = value.astype(bf16)
        if k == 0:
            get_w.wait()
        get_g[2 * k].wait()
        get_g[2 * k + 1].wait()
        back_hidden = nn(gbuf[rows], wbuf[...].reshape(1024, 512)) * hid_scale
        pbuf[rows] = (back_hidden * slope).astype(bf16)
        back = nt(pbuf[rows], ubuf[...].reshape(1024, 512)) * in_scale
        obuf[k] = back[:128]
        sbuf[k] = back[128:].astype(bf16)
        put.append(copies.start(obuf.at[k], own.at[k]))
        put.append(copies.start(sbuf.at[k], send.at[k]))
    for i in range(4):
        cols = pl.ds(i * 256, 256)
        some = pl.ds(i * 8, 8)
        grad = tn(gbuf[:, cols], hbuf[...]) * (inner_rate * hid_scale)
        outbuf[some, 1] = grad.astype(bf16).reshape(8, 32, 512)
        grad = tn(nbuf[:, cols], pbuf[...]) * (inner_rate * in_scale)
        outbuf[some, 0] = grad.astype(bf16).reshape(8, 32, 512)
        put.append(copies.start(outbuf.at[some], grads.at[some]))
    for copy in put:
        copy.wait()


def second_both(normed, cots, came, scales):
    shapes = [((4, 128, 1024), f32), ((4, 128, 1024), bf16), ((32, 2, 32, 512), bf16)]
    return pl.pallas_call(
        functools.partial(second_kernel, scales),
        out_shape=[jax.ShapeDtypeStruct(*s) for s in shapes],
        in_specs=[ANY] * 17,
        out_specs=[ANY] * 3,
        scratch_shapes=[
            pltpu.VMEM((1024, 1024), bf16),
            pltpu.VMEM((1024, 1024), bf16),
            pltpu.VMEM((32, 32, 512), bf16),
            pltpu.VMEM((32, 32, 512), bf16),
            pltpu.VMEM(*shapes[0]),
            pltpu.VMEM(*shapes[1]),
            pltpu.VMEM((1024, 512), bf16),
            pltpu.VMEM((1024, 512), bf16),
            pltpu.VMEM(*shapes[2]),
            pltpu.SemaphoreType.DMA((30,)),
        ],
        compiler_params=params(18),
        cost_estimate=cost(5 * 2 * 1024 * 1024 * 512, 11 << 20),
        name="second_both",
    )(*normed, *cots, came)


def back_kernel(scales, *refs):
    in_scale, hid_scale = scales
    n = 8
    backs, normed, came, hidden, slope = refs[:n], refs[n : 2 * n], refs[2 * n], refs[2 * n + 1], refs[2 * n + 2]
    grads = refs[2 * n + 3]
    bbuf, nbuf, wbuf, hbuf, dbuf, pbuf, outbuf, sems = refs[2 * n + 4 :]
    copies = Copies(sems)
    get_w = copies.start(came.at[:, 1], wbuf)
    get_b, get_d = [], []
    for k in range(4):
        for i in (2 * k, 2 * k + 1):
            get_b.append(copies.start(backs[i], bbuf.at[pl.ds(i * 128, 128)]))
        get_d.append(copies.start(slope.at[k], dbuf.at[pl.ds(k * 256, 256)]))
    get_h = copies.start(hidden, hbuf)
    get_n = [copies.start(normed[i], nbuf.at[pl.ds(i * 128, 128)]) for i in range(n)]
    get_w.wait()
    for k in range(4):
        rows = pl.ds(k * 256, 256)
        get_b[2 * k].wait()
        get_b[2 * k + 1].wait()
        get_d[k].wait()
        back_hidden = nn(bbuf[rows], wbuf[...].reshape(1024, 512)) * hid_scale
        pbuf[rows] = (back_hidden * dbuf[rows]).astype(bf16)
    get_h.wait()
    for copy in get_n:
        copy.wait()
    put = []
    for i in range(4):
        cols = pl.ds(i * 256, 256)
        some = pl.ds(i * 8, 8)
        grad = tn(bbuf[:, cols], hbuf[...].reshape(1024, 512)) * (inner_rate * hid_scale)
        outbuf[some, 1] = grad.astype(bf16).reshape(8, 32, 512)
        grad = tn(nbuf[:, cols], pbuf[...]) * (inner_rate * in_scale)
        outbuf[some, 0] = grad.astype(bf16).reshape(8, 32, 512)
        put.append(copies.start(outbuf.at[some], grads.at[some]))
    for copy in put:
        copy.wait()


def first_back(backs, normed, came, hidden, slope, scales):
    return pl.pallas_call(
        functools.partial(back_kernel, scales),
        out_shape=jax.ShapeDtypeStruct((32, 2, 32, 512), bf16),
        in_specs=[ANY] * 19,
        out_specs=ANY,
        scratch_shapes=[
            pltpu.VMEM((1024, 1024), bf16),
            pltpu.VMEM((1024, 1024), bf16),
            pltpu.VMEM((32, 32, 512), bf16),
            pltpu.VMEM((4, 256, 512), bf16),
            pltpu.VMEM((1024, 512), f32),
            pltpu.VMEM((1024, 512), bf16),
            pltpu.VMEM((32, 2, 32, 512), bf16),
            pltpu.SemaphoreType.DMA((30,)),
        ],
        compiler_params=params(16),
        cost_estimate=cost(3 * 2 * 1024 * 1024 * 512, 10 << 20),
        name="first_back",
    )(*backs, *normed, came, hidden, slope)


def pair_kernel(own, got, first, *rest):
    first[...] = own[0] + got[0].astype(f32)
    for k in range(1, 4):
        rest[k - 1][...] = (own[k] + got[k].astype(f32)).astype(bf16)


def pair_sum(own, got):
    block = own.shape[1:]
    return pl.pallas_call(
        pair_kernel,
        out_shape=[jax.ShapeDtypeStruct(block, f32)] + [jax.ShapeDtypeStruct(block, bf16)] * 3,
        in_specs=[VMEM] * 2,
        out_specs=[VMEM] * 4,
        compiler_params=params(20),
        cost_estimate=cost(1 << 20, 5 << 20),
        name="pair_sum",
    )(own, got)


def middle_kernel(tokens, total, one, two, three, middle, normed):
    value = total[...] + one[...].astype(f32) + two[...].astype(f32) + three[...].astype(f32)
    value = value + tokens[...].astype(f32)
    middle[...] = value
    normed[...] = (value * row_scale(value)).astype(bf16)


def middle_step(tokens, parts):
    return pl.pallas_call(
        middle_kernel,
        out_shape=[jax.ShapeDtypeStruct(tokens.shape, f32), jax.ShapeDtypeStruct(tokens.shape, bf16)],
        in_specs=[VMEM] * 5,
        out_specs=[VMEM] * 2,
        compiler_params=params(20),
        cost_estimate=cost(1 << 20, 2 << 20),
        name="middle_step",
    )(tokens, *parts)


def norm_back_kernel(cots, middle, total, one, two, three, out):
    back = total[...] + one[...].astype(f32) + two[...].astype(f32) + three[...].astype(f32)
    scale = row_scale(middle[...])
    unit = middle[...] * scale
    centred = back - unit * jnp.mean(back * unit, axis=-1, keepdims=True)
    out[...] = (cots[...].astype(f32) + scale * centred).astype(bf16)


def norm_back(cots, middle, parts):
    return pl.pallas_call(
        norm_back_kernel,
        out_shape=jax.ShapeDtypeStruct(cots.shape, bf16),
        in_specs=[VMEM] * 6,
        out_specs=VMEM,
        compiler_params=params(20),
        cost_estimate=cost(1 << 20, 3 << 20),
        name="norm_back",
    )(cots, middle, *parts)


def chip_shift(by, chips):
    return [(y * CORES + c, ((y + by) % chips) * CORES + c) for y in range(chips) for c in range(CORES)]


def other_core(chips):
    return [(i, i ^ 1) for i in range(chips * CORES)]


def gather_blocks(own, chips):
    held = [own] + [lax.ppermute(own, "fsdp", chip_shift(-k, chips)) for k in range(1, chips)]
    other = [lax.ppermute(v, "fsdp", other_core(chips)) for v in held]
    return [v for pair in zip(held, other) for v in pair]


def sum_blocks(own, send, chips):
    got = lax.ppermute(send, "fsdp", other_core(chips))
    parts = pair_sum(own, got)
    return [parts[0]] + [lax.ppermute(parts[k], "fsdp", chip_shift(k, chips)) for k in range(1, chips)]


def outer_kernel(level, given, share, came, up_w, down_w, up_m, down_m, *refs):
    outs = refs[given : given + 4]
    cbuf, wbuf, mbuf, total, wout, mout, counts, sems = refs[given + 4 :]
    paths, mods = cbuf.shape[0], wbuf.shape[1]
    half = pl.ds(level * mods, mods)
    copies = Copies(sems)
    get_c = copies.start(came, cbuf)
    get = [copies.start(v.at[half], b.at[i]) for b, pair in ((wbuf, (up_w, down_w)), (mbuf, (up_m, down_m))) for i, v in enumerate(pair)]
    for m in range(mods):
        counts[m] = 0
    total[...] = jnp.zeros_like(total)
    for p in range(paths):
        m = share[p, level] - level * mods
        counts[m] = counts[m] + 1
    get_c.wait()

    def add(p, carry):
        m = share[p, level] - level * mods
        total[m] += cbuf[p].astype(f32)
        return carry

    lax.fori_loop(0, paths, add, 0)
    for copy in get:
        copy.wait()

    def step(m, carry):
        mean = total[m] / counts[m].astype(f32)
        moment = keep_rate * mbuf[:, m].astype(f32) + mean
        weight = wbuf[:, m].astype(f32) - outer_rate * (mean + keep_rate * moment)
        wout[:, m] = weight.astype(bf16)
        mout[:, m] = moment.astype(bf16)
        return carry

    lax.fori_loop(0, mods, step, 0)
    put = [copies.start(b.at[i], outs[2 * j + i].at[half]) for j, b in enumerate((wout, mout)) for i in range(2)]
    for copy in put:
        copy.wait()


def outer_level(sharing, came, weights, moments, level, before):
    up_w, down_w = weights
    mods = up_w.shape[0] // 2
    half = (2, mods) + up_w.shape[1:]
    given = len(before)
    return pl.pallas_call(
        functools.partial(outer_kernel, level, given),
        out_shape=[jax.ShapeDtypeStruct(up_w.shape, bf16)] * 4,
        in_specs=[SMEM] + [ANY] * (5 + given),
        out_specs=[ANY] * 4,
        input_output_aliases={6 + i: i for i in range(given)},
        scratch_shapes=[
            pltpu.VMEM(came.shape, bf16),
            pltpu.VMEM(half, bf16),
            pltpu.VMEM(half, bf16),
            pltpu.VMEM((mods,) + came.shape[1:], f32),
            pltpu.VMEM(half, bf16),
            pltpu.VMEM(half, bf16),
            pltpu.SMEM((mods,), jnp.int32),
            pltpu.SemaphoreType.DMA((9,)),
        ],
        compiler_params=params(20),
        cost_estimate=cost(8 << 20, 6 << 20),
        name=f"outer_{level}",
    )(sharing, came, *weights, *moments, *before)


def exchange(values):
    return lax.all_to_all(values, "path", split_axis=0, concat_axis=0, tiled=True)


def body(hidden_in, cotangent, up_weight, down_weight, up_moment, down_moment, sharing):
    depth = up_weight.shape[1] * lax.axis_size("path")
    width = up_weight.shape[2] * lax.axis_size("fsdp")
    chips = lax.axis_size("fsdp") // CORES
    scales = (1.0 / math.sqrt(depth), 1.0 / math.sqrt(width))
    tokens, cots = hidden_in[0], cotangent[0]
    weights, moments = (up_weight, down_weight), (up_moment, down_moment)

    came_first = exchange(pick(sharing, *weights, 0))
    tokens_wide = tokens.astype(f32)
    normed_first = gather_blocks((tokens_wide * row_scale(tokens_wide)).astype(bf16), chips)
    cots_all = gather_blocks(cots, chips)
    rows_second, normed_first, cots_all = lax.optimization_barrier(
        (pick(sharing, *weights, 1), normed_first, cots_all)
    )
    came_second = exchange(rows_second)

    own, send, hidden, slope = first_forward(normed_first, came_first, scales)
    middle, normed_own = middle_step(tokens, sum_blocks(own, send, chips))
    normed_second = gather_blocks(normed_own, chips)

    own, send, grads_second = second_both(normed_second, cots_all, came_second, scales)
    back_second = exchange(grads_second)
    back_own = norm_back(cots, middle, sum_blocks(own, send, chips))
    back_middle = gather_blocks(back_own, chips)

    grads_first = first_back(back_middle, normed_first, came_first, hidden, slope, scales)
    back_first = exchange(grads_first)
    done = outer_level(sharing, back_second, weights, moments, 1, [])
    new_up, new_down, new_up_moment, new_down_moment = outer_level(
        sharing, back_first, weights, moments, 0, done
    )
    return (new_up, new_down, new_up_moment, new_down_moment)


def solution(mesh):
    tokens, pieces = P("path", "fsdp", None), P(None, "path", "fsdp")
    return jax.shard_map(
        body,
        mesh=mesh,
        in_specs=(tokens, tokens, pieces, pieces, pieces, pieces, P()),
        out_specs=(pieces,) * 4,
        check_vma=False,
    )
```

```python
import functools
import math

import jax
import jax.numpy as jnp
from jax import lax
from jax.experimental import pallas as pl
from jax.experimental.pallas import tpu as pltpu
from jax.sharding import PartitionSpec as P

inner_rate = 2.0
outer_rate = 0.7
keep_rate = 0.9
norm_eps = 1e-06
tanh_coeff = 0.7978845608028654
cube_coeff = 0.044715

f32 = jnp.float32
bf16 = jnp.bfloat16
HBM = pl.BlockSpec(memory_space=pl.ANY)
SMEM = pl.BlockSpec(memory_space=pltpu.SMEM)
VMEM = pl.BlockSpec(memory_space=pltpu.VMEM)
CORES = 2


def gelu_both(values):
    square = values * values
    tangent = jnp.tanh(tanh_coeff * (values + cube_coeff * values * square))
    half = 0.5 * (1.0 + tangent)
    slope = half + 0.5 * values * (1.0 - tangent * tangent) * tanh_coeff * (
        1.0 + 3.0 * cube_coeff * square
    )
    return (values * half, slope)


def row_scale(values):
    return lax.rsqrt(jnp.mean(values * values, axis=-1, keepdims=True) + norm_eps)


def nn(left, right):
    return jnp.dot(left, right, preferred_element_type=f32)


def nt(left, right):
    return lax.dot_general(left, right, (((1,), (1,)), ((), ())), preferred_element_type=f32)


def tn(left, right):
    return lax.dot_general(left, right, (((0,), (0,)), ((), ())), preferred_element_type=f32)


def params(mib):
    return pltpu.CompilerParams(vmem_limit_bytes=mib * 1024 * 1024)


def cost(flops, moved):
    return pl.CostEstimate(flops=flops, bytes_accessed=moved, transcendentals=0)


class Copies:
    def __init__(self, sems):
        self.sems, self.used = sems, 0

    def start(self, source, target):
        copy = pltpu.make_async_copy(source, target, self.sems.at[self.used])
        self.used += 1
        copy.start()
        return copy


def pick_kernel(level, share, up_w, down_w, out, buf, sems):
    paths = out.shape[0]
    copies = Copies(sems)
    got = []
    for p in range(paths):
        module = share[level, p]
        got.append(copies.start(up_w.at[module], buf.at[p, 0]))
        got.append(copies.start(down_w.at[module], buf.at[p, 1]))
    put = []
    for p in range(0, paths, 4):
        for copy in got[2 * p : 2 * p + 8]:
            copy.wait()
        some = pl.ds(p, 4)
        put.append(copies.start(buf.at[some], out.at[some]))
    for copy in put:
        copy.wait()


def pick(sharing, up_w, down_w, level):
    paths = sharing.shape[1]
    rows, cols = up_w.shape[1:]
    return pl.pallas_call(
        functools.partial(pick_kernel, level),
        out_shape=jax.ShapeDtypeStruct((paths, 2, rows, cols), bf16),
        in_specs=[SMEM, HBM, HBM],
        out_specs=HBM,
        scratch_shapes=[
            pltpu.VMEM((paths, 2, rows, cols), bf16),
            pltpu.SemaphoreType.DMA((2 * paths + paths // 4,)),
        ],
        compiler_params=params(60),
        cost_estimate=cost(0, 4 * paths * rows * cols * 2),
        name=f"pick_{level}",
    )(sharing, up_w, down_w)


def first_kernel(scales, *refs):
    in_scale, hid_scale = scales
    n = 8
    normed, came = refs[:n], refs[n]
    own, send, hidden, slope = refs[n + 1 : n + 5]
    nbuf, ubuf, wbuf, obuf, sbuf, hbuf, dbuf, sems = refs[n + 5 :]
    copies = Copies(sems)

    def fetch(i):
        return copies.start(normed[i], nbuf.at[i // 2, pl.ds((i % 2) * 128, 128)])

    get = [copies.start(came.at[:, 0], ubuf), fetch(0), fetch(1)]
    for copy in get:
        copy.wait()
    get_n = [fetch(i) for i in range(2, n)]
    get_w = copies.start(came.at[:, 1], wbuf)
    put = []
    for k in range(4):
        if k:
            get_n[2 * k - 2].wait()
            get_n[2 * k - 1].wait()
        value, back = gelu_both(nn(nbuf[k], ubuf[...].reshape(1024, 512)) * in_scale)
        hbuf[k] = value.astype(bf16)
        dbuf[k] = back
        put.append(copies.start(hbuf.at[k], hidden.at[k]))
        put.append(copies.start(dbuf.at[k], slope.at[k]))
    get_w.wait()
    for k in range(4):
        branch = nt(hbuf[k], wbuf[...].reshape(1024, 512)) * hid_scale
        obuf[k] = branch[:128]
        sbuf[k] = branch[128:].astype(bf16)
        put.append(copies.start(sbuf.at[k], send.at[k]))
        put.append(copies.start(obuf.at[k], own.at[k]))
    for copy in put:
        copy.wait()


def first_forward(normed, came, scales):
    shapes = [((4, 128, 1024), f32), ((4, 128, 1024), bf16), ((4, 256, 512), bf16), ((4, 256, 512), f32)]
    return pl.pallas_call(
        functools.partial(first_kernel, scales),
        out_shape=[jax.ShapeDtypeStruct(*s) for s in shapes],
        in_specs=[HBM] * 9,
        out_specs=[HBM] * 4,
        scratch_shapes=[
            pltpu.VMEM((4, 256, 1024), bf16),
            pltpu.VMEM((32, 32, 512), bf16),
            pltpu.VMEM((32, 32, 512), bf16),
        ]
        + [pltpu.VMEM(*s) for s in shapes]
        + [pltpu.SemaphoreType.DMA((26,))],
        compiler_params=params(60),
        cost_estimate=cost(2 * 2 * 1024 * 1024 * 512, 10 << 20),
        name="first_forward",
    )(*normed, came)


def second_kernel(scales, *refs):
    in_scale, hid_scale = scales
    n = 8
    normed, cots, came = refs[:n], refs[n : 2 * n], refs[2 * n]
    own, send, grads = refs[2 * n + 1 : 2 * n + 4]
    nbuf, gbuf, ubuf, wbuf, obuf, sbuf, hbuf, pbuf, dbuf, outbuf, sems = refs[2 * n + 4 :]
    copies = Copies(sems)

    def fetch(sources, target, i):
        return copies.start(sources[i], target.at[pl.ds(i * 128, 128)])

    get = [copies.start(came.at[:, 0], ubuf), fetch(normed, nbuf, 0), fetch(normed, nbuf, 1)]
    for copy in get:
        copy.wait()
    get_n = [fetch(normed, nbuf, i) for i in range(2, n)]
    get_w = copies.start(came.at[:, 1], wbuf)
    get_g = [fetch(cots, gbuf, i) for i in range(n)]
    put = []
    for k in range(4):
        rows = pl.ds(k * 256, 256)
        if k:
            get_n[2 * k - 2].wait()
            get_n[2 * k - 1].wait()
        value, slope = gelu_both(nn(nbuf[rows], ubuf[...].reshape(1024, 512)) * in_scale)
        hbuf[rows] = value.astype(bf16)
        dbuf[rows] = slope
    get_w.wait()
    for k in range(4):
        rows = pl.ds(k * 256, 256)
        get_g[2 * k].wait()
        get_g[2 * k + 1].wait()
        back_hidden = nn(gbuf[rows], wbuf[...].reshape(1024, 512)) * hid_scale
        pbuf[rows] = (back_hidden * dbuf[rows]).astype(bf16)
    for k in range(4):
        rows = pl.ds(k * 256, 256)
        back = nt(pbuf[rows], ubuf[...].reshape(1024, 512)) * in_scale
        obuf[k] = back[:128]
        sbuf[k] = back[128:].astype(bf16)
        put.append(copies.start(sbuf.at[k], send.at[k]))
        put.append(copies.start(obuf.at[k], own.at[k]))
    for i in range(4):
        cols = pl.ds(i * 256, 256)
        some = pl.ds(i * 8, 8)
        grad = tn(gbuf[:, cols], hbuf[...]) * (inner_rate * hid_scale)
        outbuf[some, 1] = grad.astype(bf16).reshape(8, 32, 512)
        grad = tn(nbuf[:, cols], pbuf[...]) * (inner_rate * in_scale)
        outbuf[some, 0] = grad.astype(bf16).reshape(8, 32, 512)
        put.append(copies.start(outbuf.at[some], grads.at[some]))
    for copy in put:
        copy.wait()


def second_both(normed, cots, came, scales):
    shapes = [((4, 128, 1024), f32), ((4, 128, 1024), bf16), ((32, 2, 32, 512), bf16)]
    return pl.pallas_call(
        functools.partial(second_kernel, scales),
        out_shape=[jax.ShapeDtypeStruct(*s) for s in shapes],
        in_specs=[HBM] * 17,
        out_specs=[HBM] * 3,
        scratch_shapes=[
            pltpu.VMEM((1024, 1024), bf16),
            pltpu.VMEM((1024, 1024), bf16),
            pltpu.VMEM((32, 32, 512), bf16),
            pltpu.VMEM((32, 32, 512), bf16),
            pltpu.VMEM(*shapes[0]),
            pltpu.VMEM(*shapes[1]),
            pltpu.VMEM((1024, 512), bf16),
            pltpu.VMEM((1024, 512), bf16),
            pltpu.VMEM((1024, 512), f32),
            pltpu.VMEM(*shapes[2]),
            pltpu.SemaphoreType.DMA((30,)),
        ],
        compiler_params=params(60),
        cost_estimate=cost(5 * 2 * 1024 * 1024 * 512, 11 << 20),
        name="second_both",
    )(*normed, *cots, came)


def back_kernel(scales, *refs):
    in_scale, hid_scale = scales
    n = 8
    backs, normed, came, hidden, slope = refs[:n], refs[n : 2 * n], refs[2 * n], refs[2 * n + 1], refs[2 * n + 2]
    grads = refs[2 * n + 3]
    bbuf, nbuf, wbuf, hbuf, dbuf, pbuf, outbuf, sems = refs[2 * n + 4 :]
    copies = Copies(sems)

    def fetch(sources, target, i):
        return copies.start(sources[i], target.at[pl.ds(i * 128, 128)])

    def fetch_slope(k):
        return copies.start(slope.at[k], dbuf.at[pl.ds(k * 256, 256)])

    get_w = copies.start(came.at[:, 1], wbuf)
    get = [[fetch(backs, bbuf, 2 * k), fetch(backs, bbuf, 2 * k + 1), fetch_slope(k)] for k in range(4)]
    get_h = copies.start(hidden, hbuf)
    get_n = [fetch(normed, nbuf, i) for i in range(n)]
    get_w.wait()
    for k in range(4):
        rows = pl.ds(k * 256, 256)
        for copy in get[k]:
            copy.wait()
        back_hidden = nn(bbuf[rows], wbuf[...].reshape(1024, 512)) * hid_scale
        pbuf[rows] = (back_hidden * dbuf[rows]).astype(bf16)
    get_h.wait()
    for copy in get_n:
        copy.wait()
    put = []
    for i in range(4):
        cols = pl.ds(i * 256, 256)
        some = pl.ds(i * 8, 8)
        grad = tn(bbuf[:, cols], hbuf[...].reshape(1024, 512)) * (inner_rate * hid_scale)
        outbuf[some, 1] = grad.astype(bf16).reshape(8, 32, 512)
        grad = tn(nbuf[:, cols], pbuf[...]) * (inner_rate * in_scale)
        outbuf[some, 0] = grad.astype(bf16).reshape(8, 32, 512)
        put.append(copies.start(outbuf.at[some], grads.at[some]))
    for copy in put:
        copy.wait()


def first_back(backs, normed, came, hidden, slope, scales):
    return pl.pallas_call(
        functools.partial(back_kernel, scales),
        out_shape=jax.ShapeDtypeStruct((32, 2, 32, 512), bf16),
        in_specs=[HBM] * 19,
        out_specs=HBM,
        scratch_shapes=[
            pltpu.VMEM((1024, 1024), bf16),
            pltpu.VMEM((1024, 1024), bf16),
            pltpu.VMEM((32, 32, 512), bf16),
            pltpu.VMEM((4, 256, 512), bf16),
            pltpu.VMEM((1024, 512), f32),
            pltpu.VMEM((1024, 512), bf16),
            pltpu.VMEM((32, 2, 32, 512), bf16),
            pltpu.SemaphoreType.DMA((30,)),
        ],
        compiler_params=params(60),
        cost_estimate=cost(3 * 2 * 1024 * 1024 * 512, 10 << 20),
        name="first_back",
    )(*backs, *normed, came, hidden, slope)


def pair_kernel(own, got, first, *rest):
    first[...] = own[0] + got[0].astype(f32)
    for k in range(1, 4):
        rest[k - 1][...] = (own[k] + got[k].astype(f32)).astype(bf16)


def pair_sum(own, got):
    block = own.shape[1:]
    return pl.pallas_call(
        pair_kernel,
        out_shape=[jax.ShapeDtypeStruct(block, f32)] + [jax.ShapeDtypeStruct(block, bf16)] * 3,
        in_specs=[VMEM] * 2,
        out_specs=[VMEM] * 4,
        compiler_params=params(12),
        cost_estimate=cost(1 << 20, 5 << 20),
        name="pair_sum",
    )(own, got)


def middle_kernel(tokens, total, one, two, three, middle, normed):
    value = total[...] + one[...].astype(f32) + two[...].astype(f32) + three[...].astype(f32)
    value = value + tokens[...].astype(f32)
    middle[...] = value
    normed[...] = (value * row_scale(value)).astype(bf16)


def middle_step(tokens, parts):
    return pl.pallas_call(
        middle_kernel,
        out_shape=[jax.ShapeDtypeStruct(tokens.shape, f32), jax.ShapeDtypeStruct(tokens.shape, bf16)],
        in_specs=[VMEM] * 5,
        out_specs=[VMEM] * 2,
        compiler_params=params(12),
        cost_estimate=cost(1 << 20, 2 << 20),
        name="middle_step",
    )(tokens, *parts)


def norm_back_kernel(cots, middle, total, one, two, three, out):
    back = total[...] + one[...].astype(f32) + two[...].astype(f32) + three[...].astype(f32)
    scale = row_scale(middle[...])
    unit = middle[...] * scale
    centred = back - unit * jnp.mean(back * unit, axis=-1, keepdims=True)
    out[...] = (cots[...].astype(f32) + scale * centred).astype(bf16)


def norm_back(cots, middle, parts):
    return pl.pallas_call(
        norm_back_kernel,
        out_shape=jax.ShapeDtypeStruct(cots.shape, bf16),
        in_specs=[VMEM] * 6,
        out_specs=VMEM,
        compiler_params=params(12),
        cost_estimate=cost(1 << 20, 3 << 20),
        name="norm_back",
    )(cots, middle, *parts)


def chip_shift(by, chips):
    return [(y * CORES + c, ((y + by) % chips) * CORES + c) for y in range(chips) for c in range(CORES)]


def other_core(chips):
    return [(i, i ^ 1) for i in range(chips * CORES)]


def gather_blocks(own, chips):
    held = [own] + [lax.ppermute(own, "fsdp", chip_shift(-k, chips)) for k in range(1, chips)]
    other = [lax.ppermute(v, "fsdp", other_core(chips)) for v in held]
    return [v for pair in zip(held, other) for v in pair]


def sum_blocks(own, send, chips):
    got = lax.ppermute(send, "fsdp", other_core(chips))
    parts = pair_sum(own, got)
    return [parts[0]] + [lax.ppermute(parts[k], "fsdp", chip_shift(k, chips)) for k in range(1, chips)]


def outer_kernel(level, given, share, came, up_w, down_w, up_m, down_m, *refs):
    outs = refs[given : given + 4]
    cbuf, wbuf, mbuf, total, wout, mout, counts, sems = refs[given + 4 :]
    paths, mods = cbuf.shape[1], wbuf.shape[1]
    half = pl.ds(level * mods, mods)
    copies = Copies(sems)
    get = []
    for i in range(2):
        get.append([copies.start(came.at[:, i], cbuf.at[i])])
        get[i].append(copies.start((up_w, down_w)[i].at[half], wbuf.at[i]))
        get[i].append(copies.start((up_m, down_m)[i].at[half], mbuf.at[i]))
    for m in range(mods):
        counts[m] = 0
    total[...] = jnp.zeros_like(total)
    for p in range(paths):
        m = share[level, p] - level * mods
        counts[m] = counts[m] + 1
    put = []
    for i in range(2):
        for copy in get[i]:
            copy.wait()

        def add(p, carry):
            m = share[level, p] - level * mods
            total[i, m] += cbuf[i, p].astype(f32)
            return carry

        lax.fori_loop(0, paths, add, 0)

        def step(m, carry):
            mean = total[i, m] / counts[m].astype(f32)
            moment = keep_rate * mbuf[i, m].astype(f32) + mean
            weight = wbuf[i, m].astype(f32) - outer_rate * (mean + keep_rate * moment)
            wout[i, m] = weight.astype(bf16)
            mout[i, m] = moment.astype(bf16)
            return carry

        lax.fori_loop(0, mods, step, 0)
        put.append(copies.start(wout.at[i], outs[i].at[half]))
        put.append(copies.start(mout.at[i], outs[2 + i].at[half]))
    for copy in put:
        copy.wait()


def outer_level(sharing, came, weights, moments, level, before):
    up_w, down_w = weights
    mods = up_w.shape[0] // 2
    half = (2, mods) + up_w.shape[1:]
    given = len(before)
    return pl.pallas_call(
        functools.partial(outer_kernel, level, given),
        out_shape=[jax.ShapeDtypeStruct(up_w.shape, bf16)] * 4,
        in_specs=[SMEM] + [HBM] * (5 + given),
        out_specs=[HBM] * 4,
        input_output_aliases={6 + i: i for i in range(given)},
        scratch_shapes=[
            pltpu.VMEM((2, came.shape[0]) + came.shape[2:], bf16),
            pltpu.VMEM(half, bf16),
            pltpu.VMEM(half, bf16),
            pltpu.VMEM(half, f32),
            pltpu.VMEM(half, bf16),
            pltpu.VMEM(half, bf16),
            pltpu.SMEM((mods,), jnp.int32),
            pltpu.SemaphoreType.DMA((10,)),
        ],
        compiler_params=params(60),
        cost_estimate=cost(8 << 20, 6 << 20),
        name=f"outer_{level}",
    )(sharing, came, *weights, *moments, *before)


def exchange(values):
    return lax.all_to_all(values, "path", split_axis=0, concat_axis=0, tiled=True)


def body(hidden_in, cotangent, up_weight, down_weight, up_moment, down_moment, sharing):
    depth = up_weight.shape[1] * lax.axis_size("path")
    width = up_weight.shape[2] * lax.axis_size("fsdp")
    chips = lax.axis_size("fsdp") // CORES
    scales = (1.0 / math.sqrt(depth), 1.0 / math.sqrt(width))
    tokens, cots = hidden_in[0], cotangent[0]
    sharing = jnp.transpose(sharing)
    weights, moments = (up_weight, down_weight), (up_moment, down_moment)

    came_first = exchange(pick(sharing, *weights, 0))
    tokens_wide = tokens.astype(f32)
    normed_first = gather_blocks((tokens_wide * row_scale(tokens_wide)).astype(bf16), chips)
    cots_all = gather_blocks(cots, chips)
    rows_second, normed_first, cots_all = lax.optimization_barrier(
        (pick(sharing, *weights, 1), normed_first, cots_all)
    )
    came_second = exchange(rows_second)

    own, send, hidden, slope = first_forward(normed_first, came_first, scales)
    middle, normed_own = middle_step(tokens, sum_blocks(own, send, chips))
    normed_second = gather_blocks(normed_own, chips)

    own, send, grads_second = second_both(normed_second, cots_all, came_second, scales)
    back_second = exchange(grads_second)
    back_own = norm_back(cots, middle, sum_blocks(own, send, chips))
    back_middle = gather_blocks(back_own, chips)

    grads_first = first_back(back_middle, normed_first, came_first, hidden, slope, scales)
    back_first = exchange(grads_first)
    done = outer_level(sharing, back_second, weights, moments, 1, [])
    new_up, new_down, new_up_moment, new_down_moment = outer_level(
        sharing, back_first, weights, moments, 0, done
    )
    return (new_up, new_down, new_up_moment, new_down_moment)


def solution(mesh):
    tokens, pieces = P("path", "fsdp", None), P(None, "path", "fsdp")
    return jax.shard_map(
        body,
        mesh=mesh,
        in_specs=(tokens, tokens, pieces, pieces, pieces, pieces, P()),
        out_specs=(pieces,) * 4,
        check_vma=False,
    )
```

```python
import functools
import math

import jax
import jax.numpy as jnp
from jax import lax
from jax.experimental import pallas as pl
from jax.experimental.pallas import tpu as pltpu
from jax.sharding import PartitionSpec as P

inner_rate = 2.0
outer_rate = 0.7
keep_rate = 0.9
norm_eps = 1e-06
tanh_coeff = 0.7978845608028654
cube_coeff = 0.044715

f32 = jnp.float32
bf16 = jnp.bfloat16
HBM = pl.BlockSpec(memory_space=pl.ANY)
SMEM = pl.BlockSpec(memory_space=pltpu.SMEM)
VMEM = pl.BlockSpec(memory_space=pltpu.VMEM)
CORES = 2


def gelu_both(values):
    square = values * values
    tangent = jnp.tanh(tanh_coeff * (values + cube_coeff * values * square))
    half = 0.5 * (1.0 + tangent)
    slope = half + 0.5 * values * (1.0 - tangent * tangent) * tanh_coeff * (
        1.0 + 3.0 * cube_coeff * square
    )
    return (values * half, slope)


def row_scale(values):
    return lax.rsqrt(jnp.mean(values * values, axis=-1, keepdims=True) + norm_eps)


def nn(left, right):
    return jnp.dot(left, right, preferred_element_type=f32)


def nt(left, right):
    return lax.dot_general(left, right, (((1,), (1,)), ((), ())), preferred_element_type=f32)


def tn(left, right):
    return lax.dot_general(left, right, (((0,), (0,)), ((), ())), preferred_element_type=f32)


def params(mib):
    return pltpu.CompilerParams(vmem_limit_bytes=mib * 1024 * 1024)


def cost(flops, moved):
    return pl.CostEstimate(flops=flops, bytes_accessed=moved, transcendentals=0)


class Copies:
    def __init__(self, sems):
        self.sems, self.used = sems, 0

    def start(self, source, target):
        copy = pltpu.make_async_copy(source, target, self.sems.at[self.used])
        self.used += 1
        copy.start()
        return copy


def pick_kernel(level, share, up_w, down_w, out, buf, sems):
    paths = out.shape[0]
    copies = Copies(sems)
    got = []
    for p in range(paths):
        module = share[level, p]
        got.append(copies.start(up_w.at[module], buf.at[p, 0]))
        got.append(copies.start(down_w.at[module], buf.at[p, 1]))
    put = []
    for p in range(0, paths, 4):
        for copy in got[2 * p : 2 * p + 8]:
            copy.wait()
        some = pl.ds(p, 4)
        put.append(copies.start(buf.at[some], out.at[some]))
    for copy in put:
        copy.wait()


def pick(sharing, up_w, down_w, level):
    paths = sharing.shape[1]
    rows, cols = up_w.shape[1:]
    return pl.pallas_call(
        functools.partial(pick_kernel, level),
        out_shape=jax.ShapeDtypeStruct((paths, 2, rows, cols), bf16),
        in_specs=[SMEM, HBM, HBM],
        out_specs=HBM,
        scratch_shapes=[
            pltpu.VMEM((paths, 2, rows, cols), bf16),
            pltpu.SemaphoreType.DMA((2 * paths + paths // 4,)),
        ],
        compiler_params=params(60),
        cost_estimate=cost(0, 4 * paths * rows * cols * 2),
        name=f"pick_{level}",
    )(sharing, up_w, down_w)


def first_kernel(scales, *refs):
    in_scale, hid_scale = scales
    n = 8
    normed, came = refs[:n], refs[n]
    own, send, hidden, slope = refs[n + 1 : n + 5]
    nbuf, ubuf, wbuf, obuf, sbuf, hbuf, dbuf, sems = refs[n + 5 :]
    copies = Copies(sems)

    def fetch(i):
        return copies.start(normed[i], nbuf.at[i // 2, pl.ds((i % 2) * 128, 128)])

    get = [copies.start(came.at[:, 0], ubuf), fetch(0), fetch(1)]
    for copy in get:
        copy.wait()
    get_n = [fetch(i) for i in range(2, n)]
    get_w = copies.start(came.at[:, 1], wbuf)
    put = []
    for k in range(4):
        if k:
            get_n[2 * k - 2].wait()
            get_n[2 * k - 1].wait()
        value, back = gelu_both(nn(nbuf[k], ubuf[...].reshape(1024, 512)) * in_scale)
        hbuf[k] = value.astype(bf16)
        dbuf[k] = back
        put.append(copies.start(hbuf.at[k], hidden.at[k]))
        put.append(copies.start(dbuf.at[k], slope.at[k]))
    get_w.wait()
    for k in range(4):
        branch = nt(hbuf[k], wbuf[...].reshape(1024, 512)) * hid_scale
        obuf[k] = branch[:128]
        sbuf[k] = branch[128:].astype(bf16)
        put.append(copies.start(sbuf.at[k], send.at[k]))
        put.append(copies.start(obuf.at[k], own.at[k]))
    for copy in put:
        copy.wait()


def first_forward(normed, came, scales):
    shapes = [((4, 128, 1024), f32), ((4, 128, 1024), bf16), ((4, 256, 512), bf16), ((4, 256, 512), f32)]
    return pl.pallas_call(
        functools.partial(first_kernel, scales),
        out_shape=[jax.ShapeDtypeStruct(*s) for s in shapes],
        in_specs=[HBM] * 9,
        out_specs=[HBM] * 4,
        scratch_shapes=[
            pltpu.VMEM((4, 256, 1024), bf16),
            pltpu.VMEM((32, 32, 512), bf16),
            pltpu.VMEM((32, 32, 512), bf16),
        ]
        + [pltpu.VMEM(*s) for s in shapes]
        + [pltpu.SemaphoreType.DMA((26,))],
        compiler_params=params(60),
        cost_estimate=cost(2 * 2 * 1024 * 1024 * 512, 10 << 20),
        name="first_forward",
    )(*normed, came)


def second_kernel(scales, *refs):
    in_scale, hid_scale = scales
    n = 8
    normed, cots, came = refs[:n], refs[n : 2 * n], refs[2 * n]
    back_pre, grads = refs[2 * n + 1 : 2 * n + 3]
    nbuf, gbuf, ubuf, wbuf, hbuf, pbuf, dbuf, outbuf, sems = refs[2 * n + 3 :]
    copies = Copies(sems)

    def fetch(sources, target, i):
        return copies.start(sources[i], target.at[pl.ds(i * 128, 128)])

    get = [copies.start(came.at[:, 0], ubuf), fetch(normed, nbuf, 0), fetch(normed, nbuf, 1)]
    for copy in get:
        copy.wait()
    get_n = [fetch(normed, nbuf, i) for i in range(2, n)]
    get_w = copies.start(came.at[:, 1], wbuf)
    get_g = [fetch(cots, gbuf, i) for i in range(n)]
    put = []
    for k in range(4):
        rows = pl.ds(k * 256, 256)
        if k:
            get_n[2 * k - 2].wait()
            get_n[2 * k - 1].wait()
        value, slope = gelu_both(nn(nbuf[rows], ubuf[...].reshape(1024, 512)) * in_scale)
        hbuf[rows] = value.astype(bf16)
        dbuf[rows] = slope
    get_w.wait()
    for k in range(4):
        rows = pl.ds(k * 256, 256)
        get_g[2 * k].wait()
        get_g[2 * k + 1].wait()
        back_hidden = nn(gbuf[rows], wbuf[...].reshape(1024, 512)) * hid_scale
        pbuf[rows] = (back_hidden * dbuf[rows]).astype(bf16)
        put.append(copies.start(pbuf.at[rows], back_pre.at[rows]))
    for i in range(4):
        cols = pl.ds(i * 256, 256)
        some = pl.ds(i * 8, 8)
        grad = tn(gbuf[:, cols], hbuf[...]) * (inner_rate * hid_scale)
        outbuf[some, 1] = grad.astype(bf16).reshape(8, 32, 512)
        grad = tn(nbuf[:, cols], pbuf[...]) * (inner_rate * in_scale)
        outbuf[some, 0] = grad.astype(bf16).reshape(8, 32, 512)
        put.append(copies.start(outbuf.at[some], grads.at[some]))
    for copy in put:
        copy.wait()


def second_both(normed, cots, came, scales):
    shapes = [((1024, 512), bf16), ((32, 2, 32, 512), bf16)]
    return pl.pallas_call(
        functools.partial(second_kernel, scales),
        out_shape=[jax.ShapeDtypeStruct(*s) for s in shapes],
        in_specs=[HBM] * 17,
        out_specs=[HBM] * 2,
        scratch_shapes=[
            pltpu.VMEM((1024, 1024), bf16),
            pltpu.VMEM((1024, 1024), bf16),
            pltpu.VMEM((32, 32, 512), bf16),
            pltpu.VMEM((32, 32, 512), bf16),
            pltpu.VMEM((1024, 512), bf16),
            pltpu.VMEM((1024, 512), bf16),
            pltpu.VMEM((1024, 512), f32),
            pltpu.VMEM(*shapes[1]),
            pltpu.SemaphoreType.DMA((30,)),
        ],
        compiler_params=params(60),
        cost_estimate=cost(4 * 2 * 1024 * 1024 * 512, 9 << 20),
        name="second_both",
    )(*normed, *cots, came)


def second_back_kernel(scale, back_pre, came, own, send, pbuf, ubuf, obuf, sbuf, sems):
    copies = Copies(sems)
    get_u = copies.start(came.at[:, 0], ubuf)
    get_p = [copies.start(back_pre.at[pl.ds(k * 256, 256)], pbuf.at[pl.ds(k * 256, 256)]) for k in range(4)]
    get_u.wait()
    put = []
    for k in range(4):
        get_p[k].wait()
        back = nt(pbuf[pl.ds(k * 256, 256)], ubuf[...].reshape(1024, 512)) * scale
        sbuf[k] = back[128:].astype(bf16)
        put.append(copies.start(sbuf.at[k], send.at[k]))
        obuf[k] = back[:128]
        put.append(copies.start(obuf.at[k], own.at[k]))
    for copy in put:
        copy.wait()


def second_back(back_pre, came, scale):
    shapes = [((4, 128, 1024), f32), ((4, 128, 1024), bf16)]
    return pl.pallas_call(
        functools.partial(second_back_kernel, scale),
        out_shape=[jax.ShapeDtypeStruct(*s) for s in shapes],
        in_specs=[HBM] * 2,
        out_specs=[HBM] * 2,
        scratch_shapes=[pltpu.VMEM((1024, 512), bf16), pltpu.VMEM((32, 32, 512), bf16)]
        + [pltpu.VMEM(*s) for s in shapes]
        + [pltpu.SemaphoreType.DMA((13,))],
        compiler_params=params(60),
        cost_estimate=cost(2 * 1024 * 1024 * 512, 5 << 20),
        name="second_back",
    )(back_pre, came)


def back_kernel(scales, *refs):
    in_scale, hid_scale = scales
    n = 8
    backs, normed, came, hidden, slope = refs[:n], refs[n : 2 * n], refs[2 * n], refs[2 * n + 1], refs[2 * n + 2]
    grads = refs[2 * n + 3]
    bbuf, nbuf, wbuf, hbuf, dbuf, pbuf, outbuf, sems = refs[2 * n + 4 :]
    copies = Copies(sems)

    def fetch(sources, target, i):
        return copies.start(sources[i], target.at[pl.ds(i * 128, 128)])

    def fetch_slope(k):
        return copies.start(slope.at[k], dbuf.at[pl.ds(k * 256, 256)])

    get_w = copies.start(came.at[:, 1], wbuf)
    get = [[fetch(backs, bbuf, 2 * k), fetch(backs, bbuf, 2 * k + 1), fetch_slope(k)] for k in range(4)]
    get_h = copies.start(hidden, hbuf)
    get_n = [fetch(normed, nbuf, i) for i in range(n)]
    get_w.wait()
    for k in range(4):
        rows = pl.ds(k * 256, 256)
        for copy in get[k]:
            copy.wait()
        back_hidden = nn(bbuf[rows], wbuf[...].reshape(1024, 512)) * hid_scale
        pbuf[rows] = (back_hidden * dbuf[rows]).astype(bf16)
    get_h.wait()
    for copy in get_n:
        copy.wait()
    put = []
    for i in range(4):
        cols = pl.ds(i * 256, 256)
        some = pl.ds(i * 8, 8)
        grad = tn(bbuf[:, cols], hbuf[...].reshape(1024, 512)) * (inner_rate * hid_scale)
        outbuf[some, 1] = grad.astype(bf16).reshape(8, 32, 512)
        grad = tn(nbuf[:, cols], pbuf[...]) * (inner_rate * in_scale)
        outbuf[some, 0] = grad.astype(bf16).reshape(8, 32, 512)
        put.append(copies.start(outbuf.at[some], grads.at[some]))
    for copy in put:
        copy.wait()


def first_back(backs, normed, came, hidden, slope, scales):
    return pl.pallas_call(
        functools.partial(back_kernel, scales),
        out_shape=jax.ShapeDtypeStruct((32, 2, 32, 512), bf16),
        in_specs=[HBM] * 19,
        out_specs=HBM,
        scratch_shapes=[
            pltpu.VMEM((1024, 1024), bf16),
            pltpu.VMEM((1024, 1024), bf16),
            pltpu.VMEM((32, 32, 512), bf16),
            pltpu.VMEM((4, 256, 512), bf16),
            pltpu.VMEM((1024, 512), f32),
            pltpu.VMEM((1024, 512), bf16),
            pltpu.VMEM((32, 2, 32, 512), bf16),
            pltpu.SemaphoreType.DMA((30,)),
        ],
        compiler_params=params(60),
        cost_estimate=cost(3 * 2 * 1024 * 1024 * 512, 10 << 20),
        name="first_back",
    )(*backs, *normed, came, hidden, slope)


def pair_kernel(own, got, first, *rest):
    first[...] = own[0] + got[0].astype(f32)
    for k in range(1, 4):
        rest[k - 1][...] = (own[k] + got[k].astype(f32)).astype(bf16)


def pair_sum(own, got):
    block = own.shape[1:]
    return pl.pallas_call(
        pair_kernel,
        out_shape=[jax.ShapeDtypeStruct(block, f32)] + [jax.ShapeDtypeStruct(block, bf16)] * 3,
        in_specs=[VMEM] * 2,
        out_specs=[VMEM] * 4,
        compiler_params=params(12),
        cost_estimate=cost(1 << 20, 5 << 20),
        name="pair_sum",
    )(own, got)


def middle_kernel(tokens, total, one, two, three, middle, normed):
    value = total[...] + one[...].astype(f32) + two[...].astype(f32) + three[...].astype(f32)
    value = value + tokens[...].astype(f32)
    middle[...] = value
    normed[...] = (value * row_scale(value)).astype(bf16)


def middle_step(tokens, parts):
    return pl.pallas_call(
        middle_kernel,
        out_shape=[jax.ShapeDtypeStruct(tokens.shape, f32), jax.ShapeDtypeStruct(tokens.shape, bf16)],
        in_specs=[VMEM] * 5,
        out_specs=[VMEM] * 2,
        compiler_params=params(12),
        cost_estimate=cost(1 << 20, 2 << 20),
        name="middle_step",
    )(tokens, *parts)


def norm_back_kernel(cots, middle, total, one, two, three, out):
    back = total[...] + one[...].astype(f32) + two[...].astype(f32) + three[...].astype(f32)
    scale = row_scale(middle[...])
    unit = middle[...] * scale
    centred = back - unit * jnp.mean(back * unit, axis=-1, keepdims=True)
    out[...] = (cots[...].astype(f32) + scale * centred).astype(bf16)


def norm_back(cots, middle, parts):
    return pl.pallas_call(
        norm_back_kernel,
        out_shape=jax.ShapeDtypeStruct(cots.shape, bf16),
        in_specs=[VMEM] * 6,
        out_specs=VMEM,
        compiler_params=params(12),
        cost_estimate=cost(1 << 20, 3 << 20),
        name="norm_back",
    )(cots, middle, *parts)


def chip_shift(by, chips):
    return [(y * CORES + c, ((y + by) % chips) * CORES + c) for y in range(chips) for c in range(CORES)]


def other_core(chips):
    return [(i, i ^ 1) for i in range(chips * CORES)]


def gather_blocks(own, chips):
    held = [own] + [lax.ppermute(own, "fsdp", chip_shift(-k, chips)) for k in range(1, chips)]
    other = [lax.ppermute(v, "fsdp", other_core(chips)) for v in held]
    return [v for pair in zip(held, other) for v in pair]


def sum_blocks(own, send, chips):
    got = lax.ppermute(send, "fsdp", other_core(chips))
    parts = pair_sum(own, got)
    return [parts[0]] + [lax.ppermute(parts[k], "fsdp", chip_shift(k, chips)) for k in range(1, chips)]


def add_paths(level, low, share, came, total):
    def add(p, carry):
        m = share[level, p] - low
        total[m] += came[p].astype(f32)
        return carry

    total[...] = jnp.zeros_like(total)
    lax.fori_loop(0, came.shape[0], add, 0, unroll=4)


def step_modules(total, counts, old_weight, old_moment, wout, mout):
    def step(m, carry):
        mean = total[m] / counts[m].astype(f32)
        moment = keep_rate * old_moment[m].astype(f32) + mean
        weight = old_weight[m].astype(f32) - outer_rate * (mean + keep_rate * moment)
        wout[m] = weight.astype(bf16)
        mout[m] = moment.astype(bf16)
        return carry

    lax.fori_loop(0, wout.shape[0], step, 0, unroll=2)


def count_paths(level, low, share, counts):
    for m in range(counts.shape[0]):
        counts[m] = 0
    for p in range(share.shape[1]):
        m = share[level, p] - low
        counts[m] = counts[m] + 1


def outer_second_kernel(share, came, up_w, down_w, up_m, down_m, *refs):
    outs = refs[:4]
    cbuf, obuf, hbuf, total, nbuf, counts, sems = refs[4:]
    mods = counts.shape[0]
    low, high = pl.ds(0, mods), pl.ds(mods, mods)
    copies = Copies(sems)
    olds = (up_w, down_w, up_m, down_m)
    get = [copies.start(came, cbuf)] + [copies.start(v.at[high], obuf.at[i]) for i, v in enumerate(olds)]
    get += [copies.start(v.at[low], hbuf.at[i]) for i, v in enumerate(olds)]
    count_paths(1, mods, share, counts)
    for copy in get:
        copy.wait()
    put = [copies.start(hbuf.at[i], outs[i].at[low]) for i in range(4)]
    for i in range(2):
        add_paths(1, mods, share, cbuf.at[:, i], total)
        step_modules(total, counts, obuf.at[i], obuf.at[2 + i], nbuf.at[i], nbuf.at[2 + i])
        put.append(copies.start(nbuf.at[i], outs[i].at[high]))
        put.append(copies.start(nbuf.at[2 + i], outs[2 + i].at[high]))
    for copy in put:
        copy.wait()


def outer_second(sharing, came, weights, moments):
    whole = weights[0].shape
    mods = whole[0] // 2
    half = (mods,) + whole[1:]
    return pl.pallas_call(
        outer_second_kernel,
        out_shape=[jax.ShapeDtypeStruct(whole, bf16)] * 4,
        in_specs=[SMEM] + [HBM] * 5,
        out_specs=[HBM] * 4,
        scratch_shapes=[
            pltpu.VMEM(came.shape, bf16),
            pltpu.VMEM((4,) + half, bf16),
            pltpu.VMEM((4,) + half, bf16),
            pltpu.VMEM(half, f32),
            pltpu.VMEM((4,) + half, bf16),
            pltpu.SMEM((mods,), jnp.int32),
            pltpu.SemaphoreType.DMA((17,)),
        ],
        compiler_params=params(12),
        cost_estimate=cost(8 << 20, 8 << 20),
        name="outer_second",
    )(sharing, came, *weights, *moments)


def outer_first_kernel(share, came, *refs):
    olds, outs = refs[:4], refs[4:8]
    cbuf, obuf, total, nbuf, counts, sems = refs[8:]
    mods = counts.shape[0]
    low = pl.ds(0, mods)
    copies = Copies(sems)
    get = []
    for i in range(2):
        get.append([copies.start(came.at[:, i], cbuf.at[i])])
        get.append([copies.start(olds[j].at[low], obuf.at[j]) for j in (i, 2 + i)])
    count_paths(0, 0, share, counts)
    put = []
    for i in range(2):
        for copy in get[2 * i]:
            copy.wait()
        add_paths(0, 0, share, cbuf.at[i], total)
        for copy in get[2 * i + 1]:
            copy.wait()
        step_modules(total, counts, obuf.at[i], obuf.at[2 + i], nbuf.at[i], nbuf.at[2 + i])
        put.append(copies.start(nbuf.at[i], outs[i].at[low]))
        put.append(copies.start(nbuf.at[2 + i], outs[2 + i].at[low]))
    for copy in put:
        copy.wait()


def outer_first(sharing, came, before):
    whole = before[0].shape
    half = (whole[0] // 2,) + whole[1:]
    return pl.pallas_call(
        outer_first_kernel,
        out_shape=[jax.ShapeDtypeStruct(whole, bf16)] * 4,
        in_specs=[SMEM, HBM] + [HBM] * 4,
        out_specs=[HBM] * 4,
        input_output_aliases={2 + i: i for i in range(4)},
        scratch_shapes=[
            pltpu.VMEM((2, came.shape[0]) + came.shape[2:], bf16),
            pltpu.VMEM((4,) + half, bf16),
            pltpu.VMEM(half, f32),
            pltpu.VMEM((4,) + half, bf16),
            pltpu.SMEM(half[:1], jnp.int32),
            pltpu.SemaphoreType.DMA((10,)),
        ],
        compiler_params=params(12),
        cost_estimate=cost(8 << 20, 6 << 20),
        name="outer_first",
    )(sharing, came, *before)


def exchange(values):
    return lax.all_to_all(values, "path", split_axis=0, concat_axis=0, tiled=True)


def body(hidden_in, cotangent, up_weight, down_weight, up_moment, down_moment, sharing):
    depth = up_weight.shape[1] * lax.axis_size("path")
    width = up_weight.shape[2] * lax.axis_size("fsdp")
    chips = lax.axis_size("fsdp") // CORES
    scales = (1.0 / math.sqrt(depth), 1.0 / math.sqrt(width))
    tokens, cots = hidden_in[0], cotangent[0]
    sharing = jnp.transpose(sharing)
    weights, moments = (up_weight, down_weight), (up_moment, down_moment)

    came_first = exchange(pick(sharing, *weights, 0))
    tokens_wide = tokens.astype(f32)
    normed_first = gather_blocks((tokens_wide * row_scale(tokens_wide)).astype(bf16), chips)
    cots_all = gather_blocks(cots, chips)
    rows_second, normed_first, cots_all = lax.optimization_barrier(
        (pick(sharing, *weights, 1), normed_first, cots_all)
    )
    came_second = exchange(rows_second)

    own, send, hidden, slope = first_forward(normed_first, came_first, scales)
    middle, normed_own = middle_step(tokens, sum_blocks(own, send, chips))
    normed_second = gather_blocks(normed_own, chips)

    back_pre, grads_second = second_both(normed_second, cots_all, came_second, scales)
    back_second = exchange(grads_second)
    own, send = second_back(back_pre, came_second, scales[0])
    back_own = norm_back(cots, middle, sum_blocks(own, send, chips))
    back_middle = gather_blocks(back_own, chips)

    grads_first = first_back(back_middle, normed_first, came_first, hidden, slope, scales)
    back_first = exchange(grads_first)
    done = outer_second(sharing, back_second, weights, moments)
    new_up, new_down, new_up_moment, new_down_moment = outer_first(sharing, back_first, done)
    return (new_up, new_down, new_up_moment, new_down_moment)


def solution(mesh):
    tokens, pieces = P("path", "fsdp", None), P(None, "path", "fsdp")
    return jax.shard_map(
        body,
        mesh=mesh,
        in_specs=(tokens, tokens, pieces, pieces, pieces, pieces, P()),
        out_specs=(pieces,) * 4,
        check_vma=False,
    )
```

```python
import functools
import math

import jax
import jax.numpy as jnp
from jax import lax
from jax.experimental import pallas as pl
from jax.experimental.pallas import tpu as pltpu
from jax.sharding import PartitionSpec as P

inner_rate = 2.0
outer_rate = 0.7
keep_rate = 0.9
norm_eps = 1e-06
tanh_coeff = 0.7978845608028654
cube_coeff = 0.044715

f32 = jnp.float32
bf16 = jnp.bfloat16
HBM = pl.BlockSpec(memory_space=pl.ANY)
SMEM = pl.BlockSpec(memory_space=pltpu.SMEM)
VMEM = pl.BlockSpec(memory_space=pltpu.VMEM)
CORES = 2


def gelu_both(values):
    square = values * values
    tangent = jnp.tanh(tanh_coeff * (values + cube_coeff * values * square))
    half = 0.5 * (1.0 + tangent)
    slope = half + 0.5 * values * (1.0 - tangent * tangent) * tanh_coeff * (
        1.0 + 3.0 * cube_coeff * square
    )
    return (values * half, slope)


def row_scale(values):
    return lax.rsqrt(jnp.mean(values * values, axis=-1, keepdims=True) + norm_eps)


def nn(left, right):
    return jnp.dot(left, right, preferred_element_type=f32)


def nt(left, right):
    return lax.dot_general(left, right, (((1,), (1,)), ((), ())), preferred_element_type=f32)


def tn(left, right):
    return lax.dot_general(left, right, (((0,), (0,)), ((), ())), preferred_element_type=f32)


def params(mib):
    return pltpu.CompilerParams(vmem_limit_bytes=mib * 1024 * 1024)


def cost(flops, moved):
    return pl.CostEstimate(flops=flops, bytes_accessed=moved, transcendentals=0)


class Copies:
    def __init__(self, sems):
        self.sems, self.used = sems, 0

    def start(self, source, target):
        copy = pltpu.make_async_copy(source, target, self.sems.at[self.used])
        self.used += 1
        copy.start()
        return copy


def pick_kernel(level, share, up_w, down_w, out, buf, sems):
    paths = out.shape[0]
    copies = Copies(sems)
    got = []
    for p in range(paths):
        module = share[level, p]
        got.append(copies.start(up_w.at[module], buf.at[p, 0]))
        got.append(copies.start(down_w.at[module], buf.at[p, 1]))
    put = []
    for p in range(0, paths, 4):
        for copy in got[2 * p : 2 * p + 8]:
            copy.wait()
        some = pl.ds(p, 4)
        put.append(copies.start(buf.at[some], out.at[some]))
    for copy in put:
        copy.wait()


def pick(sharing, up_w, down_w, level):
    paths = sharing.shape[1]
    rows, cols = up_w.shape[1:]
    return pl.pallas_call(
        functools.partial(pick_kernel, level),
        out_shape=jax.ShapeDtypeStruct((paths, 2, rows, cols), bf16),
        in_specs=[SMEM, HBM, HBM],
        out_specs=HBM,
        scratch_shapes=[
            pltpu.VMEM((paths, 2, rows, cols), bf16),
            pltpu.SemaphoreType.DMA((2 * paths + paths // 4,)),
        ],
        compiler_params=params(60),
        cost_estimate=cost(0, 4 * paths * rows * cols * 2),
        name=f"pick_{level}",
    )(sharing, up_w, down_w)


def first_kernel(scales, *refs):
    in_scale, hid_scale = scales
    n = 8
    normed, came = refs[:n], refs[n]
    own, send, hidden, slope = refs[n + 1 : n + 5]
    nbuf, ubuf, wbuf, obuf, sbuf, hbuf, dbuf, sems = refs[n + 5 :]
    copies = Copies(sems)

    def fetch(i):
        return copies.start(normed[i], nbuf.at[i // 2, pl.ds((i % 2) * 128, 128)])

    get = [copies.start(came.at[:, 0], ubuf), fetch(0), fetch(1)]
    for copy in get:
        copy.wait()
    get_n = [fetch(i) for i in range(2, n)]
    get_w = copies.start(came.at[:, 1], wbuf)
    put = []
    for k in range(4):
        if k:
            get_n[2 * k - 2].wait()
            get_n[2 * k - 1].wait()
        value, back = gelu_both(nn(nbuf[k], ubuf[...].reshape(1024, 512)) * in_scale)
        hbuf[k] = value.astype(bf16)
        dbuf[k] = back
        put.append(copies.start(hbuf.at[k], hidden.at[k]))
        put.append(copies.start(dbuf.at[k], slope.at[k]))
    get_w.wait()
    for k in range(4):
        branch = nt(hbuf[k], wbuf[...].reshape(1024, 512)) * hid_scale
        obuf[k] = branch[:128]
        sbuf[k] = branch[128:].astype(bf16)
        put.append(copies.start(sbuf.at[k], send.at[k]))
        put.append(copies.start(obuf.at[k], own.at[k]))
    for copy in put:
        copy.wait()


def first_forward(normed, came, scales):
    shapes = [((4, 128, 1024), f32), ((4, 128, 1024), bf16), ((4, 256, 512), bf16), ((4, 256, 512), f32)]
    return pl.pallas_call(
        functools.partial(first_kernel, scales),
        out_shape=[jax.ShapeDtypeStruct(*s) for s in shapes],
        in_specs=[HBM] * 9,
        out_specs=[HBM] * 4,
        scratch_shapes=[
            pltpu.VMEM((4, 256, 1024), bf16),
            pltpu.VMEM((32, 32, 512), bf16),
            pltpu.VMEM((32, 32, 512), bf16),
        ]
        + [pltpu.VMEM(*s) for s in shapes]
        + [pltpu.SemaphoreType.DMA((26,))],
        compiler_params=params(60),
        cost_estimate=cost(2 * 2 * 1024 * 1024 * 512, 10 << 20),
        name="first_forward",
    )(*normed, came)


def second_kernel(scales, *refs):
    in_scale, hid_scale = scales
    n = 8
    normed, cots, came = refs[:n], refs[n : 2 * n], refs[2 * n]
    own, send, grads = refs[2 * n + 1 : 2 * n + 4]
    nbuf, gbuf, ubuf, wbuf, obuf, sbuf, hbuf, pbuf, dbuf, outbuf, sems = refs[2 * n + 4 :]
    copies = Copies(sems)

    def fetch(sources, target, i):
        return copies.start(sources[i], target.at[pl.ds(i * 128, 128)])

    get = [copies.start(came.at[:, 0], ubuf), fetch(normed, nbuf, 0), fetch(normed, nbuf, 1)]
    for copy in get:
        copy.wait()
    get_n = [fetch(normed, nbuf, i) for i in range(2, n)]
    get_w = copies.start(came.at[:, 1], wbuf)
    get_g = [fetch(cots, gbuf, i) for i in range(n)]
    put = []
    for k in range(4):
        rows = pl.ds(k * 256, 256)
        if k:
            get_n[2 * k - 2].wait()
            get_n[2 * k - 1].wait()
        value, slope = gelu_both(nn(nbuf[rows], ubuf[...].reshape(1024, 512)) * in_scale)
        hbuf[rows] = value.astype(bf16)
        dbuf[rows] = slope
    get_w.wait()
    for k in range(4):
        rows = pl.ds(k * 256, 256)
        get_g[2 * k].wait()
        get_g[2 * k + 1].wait()
        back_hidden = nn(gbuf[rows], wbuf[...].reshape(1024, 512)) * hid_scale
        pbuf[rows] = (back_hidden * dbuf[rows]).astype(bf16)
    for k in range(4):
        rows = pl.ds(k * 256, 256)
        back = nt(pbuf[rows], ubuf[...].reshape(1024, 512)) * in_scale
        obuf[k] = back[:128]
        sbuf[k] = back[128:].astype(bf16)
        put.append(copies.start(sbuf.at[k], send.at[k]))
        put.append(copies.start(obuf.at[k], own.at[k]))
    for i in range(4):
        cols = pl.ds(i * 256, 256)
        some = pl.ds(i * 8, 8)
        grad = tn(gbuf[:, cols], hbuf[...]) * (inner_rate * hid_scale)
        outbuf[some, 1] = grad.astype(bf16).reshape(8, 32, 512)
        grad = tn(nbuf[:, cols], pbuf[...]) * (inner_rate * in_scale)
        outbuf[some, 0] = grad.astype(bf16).reshape(8, 32, 512)
        put.append(copies.start(outbuf.at[some], grads.at[some]))
    for copy in put:
        copy.wait()


def second_both(normed, cots, came, scales):
    shapes = [((4, 128, 1024), f32), ((4, 128, 1024), bf16), ((32, 2, 32, 512), bf16)]
    return pl.pallas_call(
        functools.partial(second_kernel, scales),
        out_shape=[jax.ShapeDtypeStruct(*s) for s in shapes],
        in_specs=[HBM] * 17,
        out_specs=[HBM] * 3,
        scratch_shapes=[
            pltpu.VMEM((1024, 1024), bf16),
            pltpu.VMEM((1024, 1024), bf16),
            pltpu.VMEM((32, 32, 512), bf16),
            pltpu.VMEM((32, 32, 512), bf16),
            pltpu.VMEM(*shapes[0]),
            pltpu.VMEM(*shapes[1]),
            pltpu.VMEM((1024, 512), bf16),
            pltpu.VMEM((1024, 512), bf16),
            pltpu.VMEM((1024, 512), f32),
            pltpu.VMEM(*shapes[2]),
            pltpu.SemaphoreType.DMA((30,)),
        ],
        compiler_params=params(60),
        cost_estimate=cost(5 * 2 * 1024 * 1024 * 512, 11 << 20),
        name="second_both",
    )(*normed, *cots, came)


def back_kernel(scales, *refs):
    in_scale, hid_scale = scales
    n = 8
    backs, normed, came, hidden, slope = refs[:n], refs[n : 2 * n], refs[2 * n], refs[2 * n + 1], refs[2 * n + 2]
    grads = refs[2 * n + 3]
    bbuf, nbuf, wbuf, hbuf, dbuf, pbuf, outbuf, sems = refs[2 * n + 4 :]
    copies = Copies(sems)

    def fetch(sources, target, i):
        return copies.start(sources[i], target.at[pl.ds(i * 128, 128)])

    def fetch_slope(k):
        return copies.start(slope.at[k], dbuf.at[pl.ds(k * 256, 256)])

    get_w = copies.start(came.at[:, 1], wbuf)
    get = [[fetch(backs, bbuf, 2 * k), fetch(backs, bbuf, 2 * k + 1), fetch_slope(k)] for k in range(4)]
    get_h = copies.start(hidden, hbuf)
    get_n = [fetch(normed, nbuf, i) for i in range(n)]
    get_w.wait()
    for k in range(4):
        rows = pl.ds(k * 256, 256)
        for copy in get[k]:
            copy.wait()
        back_hidden = nn(bbuf[rows], wbuf[...].reshape(1024, 512)) * hid_scale
        pbuf[rows] = (back_hidden * dbuf[rows]).astype(bf16)
    get_h.wait()
    for copy in get_n:
        copy.wait()
    put = []
    for i in range(4):
        cols = pl.ds(i * 256, 256)
        some = pl.ds(i * 8, 8)
        grad = tn(bbuf[:, cols], hbuf[...].reshape(1024, 512)) * (inner_rate * hid_scale)
        outbuf[some, 1] = grad.astype(bf16).reshape(8, 32, 512)
        grad = tn(nbuf[:, cols], pbuf[...]) * (inner_rate * in_scale)
        outbuf[some, 0] = grad.astype(bf16).reshape(8, 32, 512)
        put.append(copies.start(outbuf.at[some], grads.at[some]))
    for copy in put:
        copy.wait()


def first_back(backs, normed, came, hidden, slope, scales):
    return pl.pallas_call(
        functools.partial(back_kernel, scales),
        out_shape=jax.ShapeDtypeStruct((32, 2, 32, 512), bf16),
        in_specs=[HBM] * 19,
        out_specs=HBM,
        scratch_shapes=[
            pltpu.VMEM((1024, 1024), bf16),
            pltpu.VMEM((1024, 1024), bf16),
            pltpu.VMEM((32, 32, 512), bf16),
            pltpu.VMEM((4, 256, 512), bf16),
            pltpu.VMEM((1024, 512), f32),
            pltpu.VMEM((1024, 512), bf16),
            pltpu.VMEM((32, 2, 32, 512), bf16),
            pltpu.SemaphoreType.DMA((30,)),
        ],
        compiler_params=params(60),
        cost_estimate=cost(3 * 2 * 1024 * 1024 * 512, 10 << 20),
        name="first_back",
    )(*backs, *normed, came, hidden, slope)


def pair_kernel(own, got, first, *rest):
    first[...] = own[0] + got[0].astype(f32)
    for k in range(1, 4):
        rest[k - 1][...] = (own[k] + got[k].astype(f32)).astype(bf16)


def pair_sum(own, got):
    block = own.shape[1:]
    return pl.pallas_call(
        pair_kernel,
        out_shape=[jax.ShapeDtypeStruct(block, f32)] + [jax.ShapeDtypeStruct(block, bf16)] * 3,
        in_specs=[VMEM] * 2,
        out_specs=[VMEM] * 4,
        compiler_params=params(12),
        cost_estimate=cost(1 << 20, 5 << 20),
        name="pair_sum",
    )(own, got)


def middle_kernel(tokens, total, one, two, three, middle, normed):
    value = total[...] + one[...].astype(f32) + two[...].astype(f32) + three[...].astype(f32)
    value = value + tokens[...].astype(f32)
    middle[...] = value
    normed[...] = (value * row_scale(value)).astype(bf16)


def middle_step(tokens, parts):
    return pl.pallas_call(
        middle_kernel,
        out_shape=[jax.ShapeDtypeStruct(tokens.shape, f32), jax.ShapeDtypeStruct(tokens.shape, bf16)],
        in_specs=[VMEM] * 5,
        out_specs=[VMEM] * 2,
        compiler_params=params(12),
        cost_estimate=cost(1 << 20, 2 << 20),
        name="middle_step",
    )(tokens, *parts)


def norm_back_kernel(cots, middle, total, one, two, three, out):
    back = total[...] + one[...].astype(f32) + two[...].astype(f32) + three[...].astype(f32)
    scale = row_scale(middle[...])
    unit = middle[...] * scale
    centred = back - unit * jnp.mean(back * unit, axis=-1, keepdims=True)
    out[...] = (cots[...].astype(f32) + scale * centred).astype(bf16)


def norm_back(cots, middle, parts):
    return pl.pallas_call(
        norm_back_kernel,
        out_shape=jax.ShapeDtypeStruct(cots.shape, bf16),
        in_specs=[VMEM] * 6,
        out_specs=VMEM,
        compiler_params=params(12),
        cost_estimate=cost(1 << 20, 3 << 20),
        name="norm_back",
    )(cots, middle, *parts)


def chip_shift(by, chips):
    return [(y * CORES + c, ((y + by) % chips) * CORES + c) for y in range(chips) for c in range(CORES)]


def other_core(chips):
    return [(i, i ^ 1) for i in range(chips * CORES)]


def gather_blocks(own, chips):
    held = [own] + [lax.ppermute(own, "fsdp", chip_shift(-k, chips)) for k in range(1, chips)]
    other = [lax.ppermute(v, "fsdp", other_core(chips)) for v in held]
    return [v for pair in zip(held, other) for v in pair]


def sum_blocks(own, send, chips):
    got = lax.ppermute(send, "fsdp", other_core(chips))
    parts = pair_sum(own, got)
    return [parts[0]] + [lax.ppermute(parts[k], "fsdp", chip_shift(k, chips)) for k in range(1, chips)]


def add_paths(level, low, share, came, total):
    def add(p, carry):
        m = share[level, p] - low
        total[m] += came[p].astype(f32)
        return carry

    total[...] = jnp.zeros_like(total)
    lax.fori_loop(0, came.shape[0], add, 0, unroll=4)


def step_modules(total, counts, old_weight, old_moment, wout, mout):
    def step(m, carry):
        mean = total[m] / counts[m].astype(f32)
        moment = keep_rate * old_moment[m].astype(f32) + mean
        weight = old_weight[m].astype(f32) - outer_rate * (mean + keep_rate * moment)
        wout[m] = weight.astype(bf16)
        mout[m] = moment.astype(bf16)
        return carry

    lax.fori_loop(0, wout.shape[0], step, 0, unroll=2)


def count_paths(level, low, share, counts):
    for m in range(counts.shape[0]):
        counts[m] = 0
    for p in range(share.shape[1]):
        m = share[level, p] - low
        counts[m] = counts[m] + 1


def outer_second_kernel(share, came, up_w, down_w, up_m, down_m, *refs):
    outs = refs[:4]
    cbuf, obuf, hbuf, total, nbuf, counts, sems = refs[4:]
    mods = counts.shape[0]
    low, high = pl.ds(0, mods), pl.ds(mods, mods)
    copies = Copies(sems)
    olds = (up_w, down_w, up_m, down_m)
    get = [copies.start(came, cbuf)] + [copies.start(v.at[high], obuf.at[i]) for i, v in enumerate(olds)]
    get += [copies.start(v.at[low], hbuf.at[i]) for i, v in enumerate(olds)]
    count_paths(1, mods, share, counts)
    for copy in get:
        copy.wait()
    put = [copies.start(hbuf.at[i], outs[i].at[low]) for i in range(4)]
    for i in range(2):
        add_paths(1, mods, share, cbuf.at[:, i], total)
        step_modules(total, counts, obuf.at[i], obuf.at[2 + i], nbuf.at[i], nbuf.at[2 + i])
        put.append(copies.start(nbuf.at[i], outs[i].at[high]))
        put.append(copies.start(nbuf.at[2 + i], outs[2 + i].at[high]))
    for copy in put:
        copy.wait()


def outer_second(sharing, came, weights, moments):
    whole = weights[0].shape
    mods = whole[0] // 2
    half = (mods,) + whole[1:]
    return pl.pallas_call(
        outer_second_kernel,
        out_shape=[jax.ShapeDtypeStruct(whole, bf16)] * 4,
        in_specs=[SMEM] + [HBM] * 5,
        out_specs=[HBM] * 4,
        scratch_shapes=[
            pltpu.VMEM(came.shape, bf16),
            pltpu.VMEM((4,) + half, bf16),
            pltpu.VMEM((4,) + half, bf16),
            pltpu.VMEM(half, f32),
            pltpu.VMEM((4,) + half, bf16),
            pltpu.SMEM((mods,), jnp.int32),
            pltpu.SemaphoreType.DMA((17,)),
        ],
        compiler_params=params(12),
        cost_estimate=cost(8 << 20, 8 << 20),
        name="outer_second",
    )(sharing, came, *weights, *moments)


def outer_first_kernel(share, came, *refs):
    olds, outs = refs[:4], refs[4:8]
    cbuf, obuf, total, nbuf, counts, sems = refs[8:]
    mods = counts.shape[0]
    low = pl.ds(0, mods)
    copies = Copies(sems)
    get = []
    for i in range(2):
        get.append([copies.start(came.at[:, i], cbuf.at[i])])
        get.append([copies.start(olds[j].at[low], obuf.at[j]) for j in (i, 2 + i)])
    count_paths(0, 0, share, counts)
    put = []
    for i in range(2):
        for copy in get[2 * i]:
            copy.wait()
        add_paths(0, 0, share, cbuf.at[i], total)
        for copy in get[2 * i + 1]:
            copy.wait()
        step_modules(total, counts, obuf.at[i], obuf.at[2 + i], nbuf.at[i], nbuf.at[2 + i])
        put.append(copies.start(nbuf.at[i], outs[i].at[low]))
        put.append(copies.start(nbuf.at[2 + i], outs[2 + i].at[low]))
    for copy in put:
        copy.wait()


def outer_first(sharing, came, before):
    whole = before[0].shape
    half = (whole[0] // 2,) + whole[1:]
    return pl.pallas_call(
        outer_first_kernel,
        out_shape=[jax.ShapeDtypeStruct(whole, bf16)] * 4,
        in_specs=[SMEM, HBM] + [HBM] * 4,
        out_specs=[HBM] * 4,
        input_output_aliases={2 + i: i for i in range(4)},
        scratch_shapes=[
            pltpu.VMEM((2, came.shape[0]) + came.shape[2:], bf16),
            pltpu.VMEM((4,) + half, bf16),
            pltpu.VMEM(half, f32),
            pltpu.VMEM((4,) + half, bf16),
            pltpu.SMEM(half[:1], jnp.int32),
            pltpu.SemaphoreType.DMA((10,)),
        ],
        compiler_params=params(12),
        cost_estimate=cost(8 << 20, 6 << 20),
        name="outer_first",
    )(sharing, came, *before)


def exchange(values):
    return lax.all_to_all(values, "path", split_axis=0, concat_axis=0, tiled=True)


def body(hidden_in, cotangent, up_weight, down_weight, up_moment, down_moment, sharing):
    depth = up_weight.shape[1] * lax.axis_size("path")
    width = up_weight.shape[2] * lax.axis_size("fsdp")
    chips = lax.axis_size("fsdp") // CORES
    scales = (1.0 / math.sqrt(depth), 1.0 / math.sqrt(width))
    tokens, cots = hidden_in[0], cotangent[0]
    sharing = jnp.transpose(sharing)
    weights, moments = (up_weight, down_weight), (up_moment, down_moment)

    came_first = exchange(pick(sharing, *weights, 0))
    tokens_wide = tokens.astype(f32)
    normed_first = gather_blocks((tokens_wide * row_scale(tokens_wide)).astype(bf16), chips)
    cots_all = gather_blocks(cots, chips)
    rows_second, normed_first, cots_all = lax.optimization_barrier(
        (pick(sharing, *weights, 1), normed_first, cots_all)
    )
    came_second = exchange(rows_second)

    own, send, hidden, slope = first_forward(normed_first, came_first, scales)
    middle, normed_own = middle_step(tokens, sum_blocks(own, send, chips))
    normed_second = gather_blocks(normed_own, chips)

    own, send, grads_second = second_both(normed_second, cots_all, came_second, scales)
    back_second = exchange(grads_second)
    back_own = norm_back(cots, middle, sum_blocks(own, send, chips))
    back_middle = gather_blocks(back_own, chips)

    grads_first = first_back(back_middle, normed_first, came_first, hidden, slope, scales)
    back_first = exchange(grads_first)
    done = outer_second(sharing, back_second, weights, moments)
    new_up, new_down, new_up_moment, new_down_moment = outer_first(sharing, back_first, done)
    return (new_up, new_down, new_up_moment, new_down_moment)


def solution(mesh):
    tokens, pieces = P("path", "fsdp", None), P(None, "path", "fsdp")
    return jax.shard_map(
        body,
        mesh=mesh,
        in_specs=(tokens, tokens, pieces, pieces, pieces, pieces, P()),
        out_specs=(pieces,) * 4,
        check_vma=False,
    )
```

```python
import functools
import math

import jax
import jax.numpy as jnp
from jax import lax
from jax.experimental import pallas as pl
from jax.experimental.pallas import tpu as pltpu
from jax.sharding import PartitionSpec as P

inner_rate = 2.0
outer_rate = 0.7
keep_rate = 0.9
norm_eps = 1e-06
tanh_coeff = 0.7978845608028654
cube_coeff = 0.044715

f32 = jnp.float32
bf16 = jnp.bfloat16
HBM = pl.BlockSpec(memory_space=pl.ANY)
SMEM = pl.BlockSpec(memory_space=pltpu.SMEM)
VMEM = pl.BlockSpec(memory_space=pltpu.VMEM)
CORES = 2


def gelu_both(values):
    square = values * values
    tangent = jnp.tanh(tanh_coeff * (values + cube_coeff * values * square))
    half = 0.5 * (1.0 + tangent)
    slope = half + 0.5 * values * (1.0 - tangent * tangent) * tanh_coeff * (
        1.0 + 3.0 * cube_coeff * square
    )
    return (values * half, slope)


def row_scale(values):
    return lax.rsqrt(jnp.mean(values * values, axis=-1, keepdims=True) + norm_eps)


def nn(left, right):
    return jnp.dot(left, right, preferred_element_type=f32)


def nt(left, right):
    return lax.dot_general(left, right, (((1,), (1,)), ((), ())), preferred_element_type=f32)


def tn(left, right):
    return lax.dot_general(left, right, (((0,), (0,)), ((), ())), preferred_element_type=f32)


def params(mib):
    return pltpu.CompilerParams(vmem_limit_bytes=mib * 1024 * 1024)


def cost(flops, moved):
    return pl.CostEstimate(flops=flops, bytes_accessed=moved, transcendentals=0)


class Copies:
    def __init__(self, sems):
        self.sems, self.used = sems, 0

    def start(self, source, target):
        copy = pltpu.make_async_copy(source, target, self.sems.at[self.used])
        self.used += 1
        copy.start()
        return copy


def pick_kernel(level, share, up_w, down_w, out, buf, sems):
    paths = out.shape[0]
    copies = Copies(sems)
    got = []
    for p in range(paths):
        module = share[level, p]
        got.append(copies.start(up_w.at[module], buf.at[p, 0]))
        got.append(copies.start(down_w.at[module], buf.at[p, 1]))
    put = []
    for p in range(0, paths, 4):
        for copy in got[2 * p : 2 * p + 8]:
            copy.wait()
        some = pl.ds(p, 4)
        put.append(copies.start(buf.at[some], out.at[some]))
    for copy in put:
        copy.wait()


def pick(sharing, up_w, down_w, level):
    paths = sharing.shape[1]
    rows, cols = up_w.shape[1:]
    return pl.pallas_call(
        functools.partial(pick_kernel, level),
        out_shape=jax.ShapeDtypeStruct((paths, 2, rows, cols), bf16),
        in_specs=[SMEM, HBM, HBM],
        out_specs=HBM,
        scratch_shapes=[
            pltpu.VMEM((paths, 2, rows, cols), bf16),
            pltpu.SemaphoreType.DMA((2 * paths + paths // 4,)),
        ],
        compiler_params=params(60),
        cost_estimate=cost(0, 4 * paths * rows * cols * 2),
        name=f"pick_{level}",
    )(sharing, up_w, down_w)


def first_kernel(scales, *refs):
    in_scale, hid_scale = scales
    n = 8
    normed, came = refs[:n], refs[n]
    own, send, hidden, slope = refs[n + 1 : n + 5]
    nbuf, ubuf, wbuf, obuf, sbuf, hbuf, dbuf, sems = refs[n + 5 :]
    copies = Copies(sems)

    def fetch(i):
        return copies.start(normed[i], nbuf.at[i // 2, pl.ds((i % 2) * 128, 128)])

    get = [copies.start(came.at[:, 0], ubuf), fetch(0), fetch(1)]
    for copy in get:
        copy.wait()
    get_n = [fetch(i) for i in range(2, n)]
    get_w = copies.start(came.at[:, 1], wbuf)
    put = []
    for k in range(4):
        if k:
            get_n[2 * k - 2].wait()
            get_n[2 * k - 1].wait()
        value, back = gelu_both(nn(nbuf[k], ubuf[...].reshape(1024, 512)) * in_scale)
        hbuf[k] = value.astype(bf16)
        dbuf[k] = back
        put.append(copies.start(hbuf.at[k], hidden.at[k]))
        put.append(copies.start(dbuf.at[k], slope.at[k]))
    get_w.wait()
    for k in range(4):
        branch = nt(hbuf[k], wbuf[...].reshape(1024, 512)) * hid_scale
        obuf[k] = branch[:128]
        sbuf[k] = branch[128:].astype(bf16)
        put.append(copies.start(sbuf.at[k], send.at[k]))
        put.append(copies.start(obuf.at[k], own.at[k]))
    for copy in put:
        copy.wait()


def first_forward(normed, came, scales):
    shapes = [((4, 128, 1024), f32), ((4, 128, 1024), bf16), ((4, 256, 512), bf16), ((4, 256, 512), f32)]
    return pl.pallas_call(
        functools.partial(first_kernel, scales),
        out_shape=[jax.ShapeDtypeStruct(*s) for s in shapes],
        in_specs=[HBM] * 9,
        out_specs=[HBM] * 4,
        scratch_shapes=[
            pltpu.VMEM((4, 256, 1024), bf16),
            pltpu.VMEM((32, 32, 512), bf16),
            pltpu.VMEM((32, 32, 512), bf16),
        ]
        + [pltpu.VMEM(*s) for s in shapes]
        + [pltpu.SemaphoreType.DMA((26,))],
        compiler_params=params(60),
        cost_estimate=cost(2 * 2 * 1024 * 1024 * 512, 10 << 20),
        name="first_forward",
    )(*normed, came)


def second_kernel(scales, *refs):
    in_scale, hid_scale = scales
    n = 8
    normed, cots, came = refs[:n], refs[n : 2 * n], refs[2 * n]
    own, send, grads = refs[2 * n + 1 : 2 * n + 4]
    nbuf, gbuf, ubuf, wbuf, obuf, sbuf, hbuf, pbuf, dbuf, outbuf, sems = refs[2 * n + 4 :]
    copies = Copies(sems)

    def fetch(sources, target, i):
        return copies.start(sources[i], target.at[pl.ds(i * 128, 128)])

    get = [copies.start(came.at[:, 0], ubuf), fetch(normed, nbuf, 0), fetch(normed, nbuf, 1)]
    for copy in get:
        copy.wait()
    get_n = [fetch(normed, nbuf, i) for i in range(2, n)]
    get_w = copies.start(came.at[:, 1], wbuf)
    get_g = [fetch(cots, gbuf, i) for i in range(n)]
    put = []
    for k in range(4):
        rows = pl.ds(k * 256, 256)
        if k:
            get_n[2 * k - 2].wait()
            get_n[2 * k - 1].wait()
        value, slope = gelu_both(nn(nbuf[rows], ubuf[...].reshape(1024, 512)) * in_scale)
        hbuf[rows] = value.astype(bf16)
        dbuf[rows] = slope
    get_w.wait()
    for k in range(4):
        rows = pl.ds(k * 256, 256)
        get_g[2 * k].wait()
        get_g[2 * k + 1].wait()
        back_hidden = nn(gbuf[rows], wbuf[...].reshape(1024, 512)) * hid_scale
        pbuf[rows] = (back_hidden * dbuf[rows]).astype(bf16)
    for k in range(4):
        rows = pl.ds(k * 256, 256)
        back = nt(pbuf[rows], ubuf[...].reshape(1024, 512)) * in_scale
        obuf[k] = back[:128]
        sbuf[k] = back[128:].astype(bf16)
        put.append(copies.start(sbuf.at[k], send.at[k]))
        put.append(copies.start(obuf.at[k], own.at[k]))
    for i in range(4):
        cols = pl.ds(i * 256, 256)
        some = pl.ds(i * 8, 8)
        grad = tn(gbuf[:, cols], hbuf[...]) * (inner_rate * hid_scale)
        outbuf[some, 1] = grad.astype(bf16).reshape(8, 32, 512)
        grad = tn(nbuf[:, cols], pbuf[...]) * (inner_rate * in_scale)
        outbuf[some, 0] = grad.astype(bf16).reshape(8, 32, 512)
        put.append(copies.start(outbuf.at[some], grads.at[some]))
    for copy in put:
        copy.wait()


def second_both(normed, cots, came, scales):
    shapes = [((4, 128, 1024), f32), ((4, 128, 1024), bf16), ((32, 2, 32, 512), bf16)]
    return pl.pallas_call(
        functools.partial(second_kernel, scales),
        out_shape=[jax.ShapeDtypeStruct(*s) for s in shapes],
        in_specs=[HBM] * 17,
        out_specs=[HBM] * 3,
        scratch_shapes=[
            pltpu.VMEM((1024, 1024), bf16),
            pltpu.VMEM((1024, 1024), bf16),
            pltpu.VMEM((32, 32, 512), bf16),
            pltpu.VMEM((32, 32, 512), bf16),
            pltpu.VMEM(*shapes[0]),
            pltpu.VMEM(*shapes[1]),
            pltpu.VMEM((1024, 512), bf16),
            pltpu.VMEM((1024, 512), bf16),
            pltpu.VMEM((1024, 512), f32),
            pltpu.VMEM(*shapes[2]),
            pltpu.SemaphoreType.DMA((30,)),
        ],
        compiler_params=params(60),
        cost_estimate=cost(5 * 2 * 1024 * 1024 * 512, 11 << 20),
        name="second_both",
    )(*normed, *cots, came)


def back_kernel(scales, *refs):
    in_scale, hid_scale = scales
    n = 8
    backs, normed, came, hidden, slope = refs[:n], refs[n : 2 * n], refs[2 * n], refs[2 * n + 1], refs[2 * n + 2]
    grads = refs[2 * n + 3]
    bbuf, nbuf, wbuf, hbuf, dbuf, pbuf, outbuf, sems = refs[2 * n + 4 :]
    copies = Copies(sems)

    def fetch(sources, target, i):
        return copies.start(sources[i], target.at[pl.ds(i * 128, 128)])

    def fetch_slope(k):
        return copies.start(slope.at[k], dbuf.at[pl.ds(k * 256, 256)])

    get_w = copies.start(came.at[:, 1], wbuf)
    get = [[fetch(backs, bbuf, 2 * k), fetch(backs, bbuf, 2 * k + 1), fetch_slope(k)] for k in range(4)]
    get_h = copies.start(hidden, hbuf)
    get_n = [fetch(normed, nbuf, i) for i in range(n)]
    get_w.wait()
    for k in range(4):
        rows = pl.ds(k * 256, 256)
        for copy in get[k]:
            copy.wait()
        back_hidden = nn(bbuf[rows], wbuf[...].reshape(1024, 512)) * hid_scale
        pbuf[rows] = (back_hidden * dbuf[rows]).astype(bf16)
    get_h.wait()
    for copy in get_n:
        copy.wait()
    put = []
    for i in range(4):
        cols = pl.ds(i * 256, 256)
        some = pl.ds(i * 8, 8)
        grad = tn(bbuf[:, cols], hbuf[...].reshape(1024, 512)) * (inner_rate * hid_scale)
        outbuf[some, 1] = grad.astype(bf16).reshape(8, 32, 512)
        grad = tn(nbuf[:, cols], pbuf[...]) * (inner_rate * in_scale)
        outbuf[some, 0] = grad.astype(bf16).reshape(8, 32, 512)
        put.append(copies.start(outbuf.at[some], grads.at[some]))
    for copy in put:
        copy.wait()


def first_back(backs, normed, came, hidden, slope, scales):
    return pl.pallas_call(
        functools.partial(back_kernel, scales),
        out_shape=jax.ShapeDtypeStruct((32, 2, 32, 512), bf16),
        in_specs=[HBM] * 19,
        out_specs=HBM,
        scratch_shapes=[
            pltpu.VMEM((1024, 1024), bf16),
            pltpu.VMEM((1024, 1024), bf16),
            pltpu.VMEM((32, 32, 512), bf16),
            pltpu.VMEM((4, 256, 512), bf16),
            pltpu.VMEM((1024, 512), f32),
            pltpu.VMEM((1024, 512), bf16),
            pltpu.VMEM((32, 2, 32, 512), bf16),
            pltpu.SemaphoreType.DMA((30,)),
        ],
        compiler_params=params(60),
        cost_estimate=cost(3 * 2 * 1024 * 1024 * 512, 10 << 20),
        name="first_back",
    )(*backs, *normed, came, hidden, slope)


def pair_kernel(own, got, first, *rest):
    first[...] = own[0] + got[0].astype(f32)
    for k in range(1, 4):
        rest[k - 1][...] = (own[k] + got[k].astype(f32)).astype(bf16)


def pair_sum(own, got):
    block = own.shape[1:]
    return pl.pallas_call(
        pair_kernel,
        out_shape=[jax.ShapeDtypeStruct(block, f32)] + [jax.ShapeDtypeStruct(block, bf16)] * 3,
        in_specs=[VMEM] * 2,
        out_specs=[VMEM] * 4,
        compiler_params=params(12),
        cost_estimate=cost(1 << 20, 5 << 20),
        name="pair_sum",
    )(own, got)


def middle_kernel(tokens, total, one, two, three, middle, normed):
    value = total[...] + one[...].astype(f32) + two[...].astype(f32) + three[...].astype(f32)
    value = value + tokens[...].astype(f32)
    middle[...] = value
    normed[...] = (value * row_scale(value)).astype(bf16)


def middle_step(tokens, parts):
    return pl.pallas_call(
        middle_kernel,
        out_shape=[jax.ShapeDtypeStruct(tokens.shape, f32), jax.ShapeDtypeStruct(tokens.shape, bf16)],
        in_specs=[VMEM] * 5,
        out_specs=[VMEM] * 2,
        compiler_params=params(12),
        cost_estimate=cost(1 << 20, 2 << 20),
        name="middle_step",
    )(tokens, *parts)


def norm_back_kernel(cots, middle, total, one, two, three, out):
    back = total[...] + one[...].astype(f32) + two[...].astype(f32) + three[...].astype(f32)
    scale = row_scale(middle[...])
    unit = middle[...] * scale
    centred = back - unit * jnp.mean(back * unit, axis=-1, keepdims=True)
    out[...] = (cots[...].astype(f32) + scale * centred).astype(bf16)


def norm_back(cots, middle, parts):
    return pl.pallas_call(
        norm_back_kernel,
        out_shape=jax.ShapeDtypeStruct(cots.shape, bf16),
        in_specs=[VMEM] * 6,
        out_specs=VMEM,
        compiler_params=params(12),
        cost_estimate=cost(1 << 20, 3 << 20),
        name="norm_back",
    )(cots, middle, *parts)


def chip_shift(by, chips):
    return [(y * CORES + c, ((y + by) % chips) * CORES + c) for y in range(chips) for c in range(CORES)]


def other_core(chips):
    return [(i, i ^ 1) for i in range(chips * CORES)]


def gather_blocks(own, chips):
    held = [own] + [lax.ppermute(own, "fsdp", chip_shift(-k, chips)) for k in range(1, chips)]
    other = [lax.ppermute(v, "fsdp", other_core(chips)) for v in held]
    return [v for pair in zip(held, other) for v in pair]


def settle_kernel(*refs):
    pass


def settle(values):
    count = len(values)
    return pl.pallas_call(
        settle_kernel,
        out_shape=[jax.ShapeDtypeStruct(v.shape, v.dtype) for v in values],
        in_specs=[HBM] * count,
        out_specs=[HBM] * count,
        input_output_aliases={i: i for i in range(count)},
        compiler_params=params(60),
        cost_estimate=cost(0, 4 << 20),
        name="settle",
    )(*values)


def sum_blocks(own, send, chips):
    got = lax.ppermute(send, "fsdp", other_core(chips))
    parts = pair_sum(own, got)
    return [parts[0]] + [lax.ppermute(parts[k], "fsdp", chip_shift(k, chips)) for k in range(1, chips)]


def add_paths(level, low, share, came, total):
    def add(p, carry):
        m = share[level, p] - low
        total[m] += came[p].astype(f32)
        return carry

    total[...] = jnp.zeros_like(total)
    lax.fori_loop(0, came.shape[0], add, 0, unroll=4)


def step_modules(total, counts, old_weight, old_moment, wout, mout):
    def step(m, carry):
        mean = total[m] / counts[m].astype(f32)
        moment = keep_rate * old_moment[m].astype(f32) + mean
        weight = old_weight[m].astype(f32) - outer_rate * (mean + keep_rate * moment)
        wout[m] = weight.astype(bf16)
        mout[m] = moment.astype(bf16)
        return carry

    lax.fori_loop(0, wout.shape[0], step, 0, unroll=2)


def count_paths(level, low, share, counts):
    for m in range(counts.shape[0]):
        counts[m] = 0
    for p in range(share.shape[1]):
        m = share[level, p] - low
        counts[m] = counts[m] + 1


def outer_second_kernel(share, came, up_w, down_w, up_m, down_m, *refs):
    outs = refs[:4]
    cbuf, obuf, hbuf, total, nbuf, counts, sems = refs[4:]
    mods = counts.shape[0]
    low, high = pl.ds(0, mods), pl.ds(mods, mods)
    copies = Copies(sems)
    olds = (up_w, down_w, up_m, down_m)
    get = [copies.start(came, cbuf)] + [copies.start(v.at[high], obuf.at[i]) for i, v in enumerate(olds)]
    get += [copies.start(v.at[low], hbuf.at[i]) for i, v in enumerate(olds)]
    count_paths(1, mods, share, counts)
    for copy in get:
        copy.wait()
    put = [copies.start(hbuf.at[i], outs[i].at[low]) for i in range(4)]
    for i in range(2):
        add_paths(1, mods, share, cbuf.at[:, i], total)
        step_modules(total, counts, obuf.at[i], obuf.at[2 + i], nbuf.at[i], nbuf.at[2 + i])
        put.append(copies.start(nbuf.at[i], outs[i].at[high]))
        put.append(copies.start(nbuf.at[2 + i], outs[2 + i].at[high]))
    for copy in put:
        copy.wait()


def outer_second(sharing, came, weights, moments):
    whole = weights[0].shape
    mods = whole[0] // 2
    half = (mods,) + whole[1:]
    return pl.pallas_call(
        outer_second_kernel,
        out_shape=[jax.ShapeDtypeStruct(whole, bf16)] * 4,
        in_specs=[SMEM] + [HBM] * 5,
        out_specs=[HBM] * 4,
        scratch_shapes=[
            pltpu.VMEM(came.shape, bf16),
            pltpu.VMEM((4,) + half, bf16),
            pltpu.VMEM((4,) + half, bf16),
            pltpu.VMEM(half, f32),
            pltpu.VMEM((4,) + half, bf16),
            pltpu.SMEM((mods,), jnp.int32),
            pltpu.SemaphoreType.DMA((17,)),
        ],
        compiler_params=params(12),
        cost_estimate=cost(8 << 20, 8 << 20),
        name="outer_second",
    )(sharing, came, *weights, *moments)


def outer_first_kernel(share, came, *refs):
    olds, outs = refs[:4], refs[4:8]
    cbuf, obuf, total, nbuf, counts, sems = refs[8:]
    mods = counts.shape[0]
    low = pl.ds(0, mods)
    copies = Copies(sems)
    get = []
    for i in range(2):
        get.append([copies.start(came.at[:, i], cbuf.at[i])])
        get.append([copies.start(olds[j].at[low], obuf.at[j]) for j in (i, 2 + i)])
    count_paths(0, 0, share, counts)
    put = []
    for i in range(2):
        for copy in get[2 * i]:
            copy.wait()
        add_paths(0, 0, share, cbuf.at[i], total)
        for copy in get[2 * i + 1]:
            copy.wait()
        step_modules(total, counts, obuf.at[i], obuf.at[2 + i], nbuf.at[i], nbuf.at[2 + i])
        put.append(copies.start(nbuf.at[i], outs[i].at[low]))
        put.append(copies.start(nbuf.at[2 + i], outs[2 + i].at[low]))
    for copy in put:
        copy.wait()


def outer_first(sharing, came, before):
    whole = before[0].shape
    half = (whole[0] // 2,) + whole[1:]
    return pl.pallas_call(
        outer_first_kernel,
        out_shape=[jax.ShapeDtypeStruct(whole, bf16)] * 4,
        in_specs=[SMEM, HBM] + [HBM] * 4,
        out_specs=[HBM] * 4,
        input_output_aliases={2 + i: i for i in range(4)},
        scratch_shapes=[
            pltpu.VMEM((2, came.shape[0]) + came.shape[2:], bf16),
            pltpu.VMEM((4,) + half, bf16),
            pltpu.VMEM(half, f32),
            pltpu.VMEM((4,) + half, bf16),
            pltpu.SMEM(half[:1], jnp.int32),
            pltpu.SemaphoreType.DMA((10,)),
        ],
        compiler_params=params(12),
        cost_estimate=cost(8 << 20, 6 << 20),
        name="outer_first",
    )(sharing, came, *before)


def exchange(values):
    return lax.all_to_all(values, "path", split_axis=0, concat_axis=0, tiled=True)


def body(hidden_in, cotangent, up_weight, down_weight, up_moment, down_moment, sharing):
    depth = up_weight.shape[1] * lax.axis_size("path")
    width = up_weight.shape[2] * lax.axis_size("fsdp")
    chips = lax.axis_size("fsdp") // CORES
    scales = (1.0 / math.sqrt(depth), 1.0 / math.sqrt(width))
    tokens, cots = hidden_in[0], cotangent[0]
    sharing = jnp.transpose(sharing)
    weights, moments = (up_weight, down_weight), (up_moment, down_moment)

    came_first = exchange(pick(sharing, *weights, 0))
    tokens_wide = tokens.astype(f32)
    normed_first = gather_blocks((tokens_wide * row_scale(tokens_wide)).astype(bf16), chips)
    cots_all = gather_blocks(cots, chips)
    rows_second, normed_first, cots_all = lax.optimization_barrier(
        (pick(sharing, *weights, 1), normed_first, cots_all)
    )
    came_second = exchange(rows_second)

    own, send, hidden, slope = first_forward(normed_first, came_first, scales)
    middle, normed_own = middle_step(tokens, sum_blocks(own, send, chips))
    normed_second = settle(gather_blocks(normed_own, chips))

    own, send, grads_second = second_both(normed_second, cots_all, came_second, scales)
    back_second = exchange(grads_second)
    back_own = norm_back(cots, middle, sum_blocks(own, send, chips))
    back_middle = gather_blocks(back_own, chips)

    grads_first = first_back(back_middle, normed_first, came_first, hidden, slope, scales)
    back_first = exchange(grads_first)
    done = outer_second(sharing, back_second, weights, moments)
    new_up, new_down, new_up_moment, new_down_moment = outer_first(sharing, back_first, done)
    return (new_up, new_down, new_up_moment, new_down_moment)


def solution(mesh):
    tokens, pieces = P("path", "fsdp", None), P(None, "path", "fsdp")
    return jax.shard_map(
        body,
        mesh=mesh,
        in_specs=(tokens, tokens, pieces, pieces, pieces, pieces, P()),
        out_specs=(pieces,) * 4,
        check_vma=False,
    )
```

```python
import functools
import math

import jax
import jax.numpy as jnp
from jax import lax
from jax.experimental import pallas as pl
from jax.experimental.pallas import tpu as pltpu
from jax.sharding import PartitionSpec as P

inner_rate = 2.0
outer_rate = 0.7
keep_rate = 0.9
norm_eps = 1e-06
tanh_coeff = 0.7978845608028654
cube_coeff = 0.044715

f32 = jnp.float32
bf16 = jnp.bfloat16
HBM = pl.BlockSpec(memory_space=pl.ANY)
SMEM = pl.BlockSpec(memory_space=pltpu.SMEM)
VMEM = pl.BlockSpec(memory_space=pltpu.VMEM)
CORES = 2


def gelu_both(values):
    square = values * values
    tangent = jnp.tanh(tanh_coeff * (values + cube_coeff * values * square))
    half = 0.5 * (1.0 + tangent)
    slope = half + 0.5 * values * (1.0 - tangent * tangent) * tanh_coeff * (
        1.0 + 3.0 * cube_coeff * square
    )
    return (values * half, slope)


def row_scale(values):
    return lax.rsqrt(jnp.mean(values * values, axis=-1, keepdims=True) + norm_eps)


def nn(left, right):
    return jnp.dot(left, right, preferred_element_type=f32)


def nt(left, right):
    return lax.dot_general(left, right, (((1,), (1,)), ((), ())), preferred_element_type=f32)


def tn(left, right):
    return lax.dot_general(left, right, (((0,), (0,)), ((), ())), preferred_element_type=f32)


def params(mib):
    return pltpu.CompilerParams(vmem_limit_bytes=mib * 1024 * 1024)


def cost(flops, moved):
    return pl.CostEstimate(flops=flops, bytes_accessed=moved, transcendentals=0)


class Copies:
    def __init__(self, sems):
        self.sems, self.used = sems, 0

    def start(self, source, target):
        copy = pltpu.make_async_copy(source, target, self.sems.at[self.used])
        self.used += 1
        copy.start()
        return copy


def pick_kernel(level, share, up_w, down_w, out, buf, sems):
    paths = out.shape[0]
    copies = Copies(sems)
    got = []
    for p in range(paths):
        module = share[level, p]
        got.append(copies.start(up_w.at[module], buf.at[p, 0]))
        got.append(copies.start(down_w.at[module], buf.at[p, 1]))
    put = []
    for p in range(0, paths, 4):
        for copy in got[2 * p : 2 * p + 8]:
            copy.wait()
        some = pl.ds(p, 4)
        put.append(copies.start(buf.at[some], out.at[some]))
    for copy in put:
        copy.wait()


def pick(sharing, up_w, down_w, level):
    paths = sharing.shape[1]
    rows, cols = up_w.shape[1:]
    return pl.pallas_call(
        functools.partial(pick_kernel, level),
        out_shape=jax.ShapeDtypeStruct((paths, 2, rows, cols), bf16),
        in_specs=[SMEM, HBM, HBM],
        out_specs=HBM,
        scratch_shapes=[
            pltpu.VMEM((paths, 2, rows, cols), bf16),
            pltpu.SemaphoreType.DMA((2 * paths + paths // 4,)),
        ],
        compiler_params=params(60),
        cost_estimate=cost(0, 4 * paths * rows * cols * 2),
        name=f"pick_{level}",
    )(sharing, up_w, down_w)


def first_kernel(scales, *refs):
    in_scale, hid_scale = scales
    n = 8
    normed, came = refs[:n], refs[n]
    own, send, hidden, slope = refs[n + 1 : n + 5]
    nbuf, ubuf, wbuf, obuf, sbuf, hbuf, dbuf, sems = refs[n + 5 :]
    copies = Copies(sems)

    def fetch(i):
        return copies.start(normed[i], nbuf.at[i // 2, pl.ds((i % 2) * 128, 128)])

    get = [copies.start(came.at[:, 0], ubuf), fetch(0), fetch(1)]
    for copy in get:
        copy.wait()
    get_n = [fetch(i) for i in range(2, n)]
    get_w = copies.start(came.at[:, 1], wbuf)
    put = []
    for k in range(4):
        if k:
            get_n[2 * k - 2].wait()
            get_n[2 * k - 1].wait()
        value, back = gelu_both(nn(nbuf[k], ubuf[...].reshape(1024, 512)) * in_scale)
        hbuf[k] = value.astype(bf16)
        dbuf[k] = back.astype(bf16)
        put.append(copies.start(hbuf.at[k], hidden.at[k]))
        put.append(copies.start(dbuf.at[k], slope.at[k]))
    get_w.wait()
    for k in range(4):
        branch = nt(hbuf[k], wbuf[...].reshape(1024, 512)) * hid_scale
        obuf[k] = branch[:128].astype(bf16)
        sbuf[k] = branch[128:].astype(bf16)
        put.append(copies.start(sbuf.at[k], send.at[k]))
        put.append(copies.start(obuf.at[k], own.at[k]))
    for copy in put:
        copy.wait()


def first_forward(normed, came, scales):
    shapes = [((4, 128, 1024), bf16), ((4, 128, 1024), bf16), ((4, 256, 512), bf16), ((4, 256, 512), bf16)]
    return pl.pallas_call(
        functools.partial(first_kernel, scales),
        out_shape=[jax.ShapeDtypeStruct(*s) for s in shapes],
        in_specs=[HBM] * 9,
        out_specs=[HBM] * 4,
        scratch_shapes=[
            pltpu.VMEM((4, 256, 1024), bf16),
            pltpu.VMEM((32, 32, 512), bf16),
            pltpu.VMEM((32, 32, 512), bf16),
        ]
        + [pltpu.VMEM(*s) for s in shapes]
        + [pltpu.SemaphoreType.DMA((26,))],
        compiler_params=params(60),
        cost_estimate=cost(2 * 2 * 1024 * 1024 * 512, 10 << 20),
        name="first_forward",
    )(*normed, came)


def second_kernel(scales, *refs):
    in_scale, hid_scale = scales
    n = 8
    normed, cots, came = refs[:n], refs[n : 2 * n], refs[2 * n]
    own, send, grads = refs[2 * n + 1 : 2 * n + 4]
    nbuf, gbuf, ubuf, wbuf, obuf, sbuf, hbuf, pbuf, dbuf, outbuf, sems = refs[2 * n + 4 :]
    copies = Copies(sems)

    def fetch(sources, target, i):
        return copies.start(sources[i], target.at[pl.ds(i * 128, 128)])

    get = [copies.start(came.at[:, 0], ubuf), fetch(normed, nbuf, 0), fetch(normed, nbuf, 1)]
    for copy in get:
        copy.wait()
    get_n = [fetch(normed, nbuf, i) for i in range(2, n)]
    get_w = copies.start(came.at[:, 1], wbuf)
    get_g = [fetch(cots, gbuf, i) for i in range(n)]
    put = []
    for k in range(4):
        rows = pl.ds(k * 256, 256)
        if k:
            get_n[2 * k - 2].wait()
            get_n[2 * k - 1].wait()
        value, slope = gelu_both(nn(nbuf[rows], ubuf[...].reshape(1024, 512)) * in_scale)
        hbuf[rows] = value.astype(bf16)
        dbuf[rows] = slope
    get_w.wait()
    for k in range(4):
        rows = pl.ds(k * 256, 256)
        get_g[2 * k].wait()
        get_g[2 * k + 1].wait()
        back_hidden = nn(gbuf[rows], wbuf[...].reshape(1024, 512)) * hid_scale
        pbuf[rows] = (back_hidden * dbuf[rows]).astype(bf16)
    for k in range(4):
        rows = pl.ds(k * 256, 256)
        back = nt(pbuf[rows], ubuf[...].reshape(1024, 512)) * in_scale
        obuf[k] = back[:128].astype(bf16)
        sbuf[k] = back[128:].astype(bf16)
        put.append(copies.start(sbuf.at[k], send.at[k]))
        put.append(copies.start(obuf.at[k], own.at[k]))
    for i in range(4):
        cols = pl.ds(i * 256, 256)
        some = pl.ds(i * 8, 8)
        grad = tn(gbuf[:, cols], hbuf[...]) * (inner_rate * hid_scale)
        outbuf[some, 1] = grad.astype(bf16).reshape(8, 32, 512)
        grad = tn(nbuf[:, cols], pbuf[...]) * (inner_rate * in_scale)
        outbuf[some, 0] = grad.astype(bf16).reshape(8, 32, 512)
        put.append(copies.start(outbuf.at[some], grads.at[some]))
    for copy in put:
        copy.wait()


def second_both(normed, cots, came, scales):
    shapes = [((4, 128, 1024), bf16), ((4, 128, 1024), bf16), ((32, 2, 32, 512), bf16)]
    return pl.pallas_call(
        functools.partial(second_kernel, scales),
        out_shape=[jax.ShapeDtypeStruct(*s) for s in shapes],
        in_specs=[HBM] * 17,
        out_specs=[HBM] * 3,
        scratch_shapes=[
            pltpu.VMEM((1024, 1024), bf16),
            pltpu.VMEM((1024, 1024), bf16),
            pltpu.VMEM((32, 32, 512), bf16),
            pltpu.VMEM((32, 32, 512), bf16),
            pltpu.VMEM(*shapes[0]),
            pltpu.VMEM(*shapes[1]),
            pltpu.VMEM((1024, 512), bf16),
            pltpu.VMEM((1024, 512), bf16),
            pltpu.VMEM((1024, 512), f32),
            pltpu.VMEM(*shapes[2]),
            pltpu.SemaphoreType.DMA((30,)),
        ],
        compiler_params=params(60),
        cost_estimate=cost(5 * 2 * 1024 * 1024 * 512, 11 << 20),
        name="second_both",
    )(*normed, *cots, came)


def back_kernel(scales, *refs):
    in_scale, hid_scale = scales
    n = 8
    backs, normed, came, hidden, slope = refs[:n], refs[n : 2 * n], refs[2 * n], refs[2 * n + 1], refs[2 * n + 2]
    grads = refs[2 * n + 3]
    bbuf, nbuf, wbuf, hbuf, dbuf, pbuf, outbuf, sems = refs[2 * n + 4 :]
    copies = Copies(sems)

    def fetch(sources, target, i):
        return copies.start(sources[i], target.at[pl.ds(i * 128, 128)])

    def fetch_slope(k):
        return copies.start(slope.at[k], dbuf.at[pl.ds(k * 256, 256)])

    get_w = copies.start(came.at[:, 1], wbuf)
    get = [[fetch(backs, bbuf, 2 * k), fetch(backs, bbuf, 2 * k + 1), fetch_slope(k)] for k in range(4)]
    get_h = copies.start(hidden, hbuf)
    get_n = [fetch(normed, nbuf, i) for i in range(n)]
    get_w.wait()
    for k in range(4):
        rows = pl.ds(k * 256, 256)
        for copy in get[k]:
            copy.wait()
        back_hidden = nn(bbuf[rows], wbuf[...].reshape(1024, 512)) * hid_scale
        pbuf[rows] = (back_hidden * dbuf[rows].astype(f32)).astype(bf16)
    get_h.wait()
    for copy in get_n:
        copy.wait()
    put = []
    for i in range(4):
        cols = pl.ds(i * 256, 256)
        some = pl.ds(i * 8, 8)
        grad = tn(bbuf[:, cols], hbuf[...].reshape(1024, 512)) * (inner_rate * hid_scale)
        outbuf[some, 1] = grad.astype(bf16).reshape(8, 32, 512)
        grad = tn(nbuf[:, cols], pbuf[...]) * (inner_rate * in_scale)
        outbuf[some, 0] = grad.astype(bf16).reshape(8, 32, 512)
        put.append(copies.start(outbuf.at[some], grads.at[some]))
    for copy in put:
        copy.wait()


def first_back(backs, normed, came, hidden, slope, scales):
    return pl.pallas_call(
        functools.partial(back_kernel, scales),
        out_shape=jax.ShapeDtypeStruct((32, 2, 32, 512), bf16),
        in_specs=[HBM] * 19,
        out_specs=HBM,
        scratch_shapes=[
            pltpu.VMEM((1024, 1024), bf16),
            pltpu.VMEM((1024, 1024), bf16),
            pltpu.VMEM((32, 32, 512), bf16),
            pltpu.VMEM((4, 256, 512), bf16),
            pltpu.VMEM((1024, 512), bf16),
            pltpu.VMEM((1024, 512), bf16),
            pltpu.VMEM((32, 2, 32, 512), bf16),
            pltpu.SemaphoreType.DMA((30,)),
        ],
        compiler_params=params(60),
        cost_estimate=cost(3 * 2 * 1024 * 1024 * 512, 10 << 20),
        name="first_back",
    )(*backs, *normed, came, hidden, slope)


def pair_kernel(own, got, first, *rest):
    first[...] = own[0].astype(f32) + got[0].astype(f32)
    for k in range(1, 4):
        rest[k - 1][...] = (own[k].astype(f32) + got[k].astype(f32)).astype(bf16)


def pair_sum(own, got):
    block = own.shape[1:]
    return pl.pallas_call(
        pair_kernel,
        out_shape=[jax.ShapeDtypeStruct(block, f32)] + [jax.ShapeDtypeStruct(block, bf16)] * 3,
        in_specs=[VMEM] * 2,
        out_specs=[VMEM] * 4,
        compiler_params=params(12),
        cost_estimate=cost(1 << 20, 5 << 20),
        name="pair_sum",
    )(own, got)


def middle_kernel(tokens, total, one, two, three, middle, normed):
    value = total[...] + one[...].astype(f32) + two[...].astype(f32) + three[...].astype(f32)
    value = value + tokens[...].astype(f32)
    middle[...] = value
    normed[...] = (value * row_scale(value)).astype(bf16)


def middle_step(tokens, parts):
    return pl.pallas_call(
        middle_kernel,
        out_shape=[jax.ShapeDtypeStruct(tokens.shape, f32), jax.ShapeDtypeStruct(tokens.shape, bf16)],
        in_specs=[VMEM] * 5,
        out_specs=[VMEM] * 2,
        compiler_params=params(12),
        cost_estimate=cost(1 << 20, 2 << 20),
        name="middle_step",
    )(tokens, *parts)


def norm_back_kernel(cots, middle, total, one, two, three, out):
    back = total[...] + one[...].astype(f32) + two[...].astype(f32) + three[...].astype(f32)
    scale = row_scale(middle[...])
    unit = middle[...] * scale
    centred = back - unit * jnp.mean(back * unit, axis=-1, keepdims=True)
    out[...] = (cots[...].astype(f32) + scale * centred).astype(bf16)


def norm_back(cots, middle, parts):
    return pl.pallas_call(
        norm_back_kernel,
        out_shape=jax.ShapeDtypeStruct(cots.shape, bf16),
        in_specs=[VMEM] * 6,
        out_specs=VMEM,
        compiler_params=params(12),
        cost_estimate=cost(1 << 20, 3 << 20),
        name="norm_back",
    )(cots, middle, *parts)


def chip_shift(by, chips):
    return [(y * CORES + c, ((y + by) % chips) * CORES + c) for y in range(chips) for c in range(CORES)]


def by_distance(chips):
    return sorted(range(1, chips), key=lambda k: -min(k, chips - k))


def other_core(chips):
    return [(i, i ^ 1) for i in range(chips * CORES)]


def gather_blocks(own, chips):
    held = {0: own}
    for k in by_distance(chips):
        held[k] = lax.ppermute(own, "fsdp", chip_shift(-k, chips))
    other = {k: lax.ppermute(v, "fsdp", other_core(chips)) for k, v in held.items()}
    return [v for k in range(chips) for v in (held[k], other[k])]


def settle_kernel(*refs):
    pass


def settle(values):
    count = len(values)
    return pl.pallas_call(
        settle_kernel,
        out_shape=[jax.ShapeDtypeStruct(v.shape, v.dtype) for v in values],
        in_specs=[HBM] * count,
        out_specs=[HBM] * count,
        input_output_aliases={i: i for i in range(count)},
        compiler_params=params(60),
        cost_estimate=cost(0, 4 << 20),
        name="settle",
    )(*values)


def sum_blocks(own, send, chips):
    got = lax.ppermute(send, "fsdp", other_core(chips))
    parts = pair_sum(own, got)
    return [parts[0]] + [lax.ppermute(parts[k], "fsdp", chip_shift(k, chips)) for k in by_distance(chips)]


def add_paths(level, low, share, came, total):
    def add(p, carry):
        m = share[level, p] - low
        total[m] += came[p].astype(f32)
        return carry

    total[...] = jnp.zeros_like(total)
    lax.fori_loop(0, came.shape[0], add, 0, unroll=4)


def step_modules(total, counts, old_weight, old_moment, wout, mout):
    def step(m, carry):
        mean = total[m] / counts[m].astype(f32)
        moment = keep_rate * old_moment[m].astype(f32) + mean
        weight = old_weight[m].astype(f32) - outer_rate * (mean + keep_rate * moment)
        wout[m] = weight.astype(bf16)
        mout[m] = moment.astype(bf16)
        return carry

    lax.fori_loop(0, wout.shape[0], step, 0, unroll=2)


def count_paths(level, low, share, counts):
    for m in range(counts.shape[0]):
        counts[m] = 0
    for p in range(share.shape[1]):
        m = share[level, p] - low
        counts[m] = counts[m] + 1


def outer_second_kernel(share, came, up_w, down_w, up_m, down_m, *refs):
    outs = refs[:4]
    cbuf, obuf, hbuf, total, nbuf, counts, sems = refs[4:]
    mods = counts.shape[0]
    low, high = pl.ds(0, mods), pl.ds(mods, mods)
    copies = Copies(sems)
    olds = (up_w, down_w, up_m, down_m)
    get = [copies.start(came, cbuf)] + [copies.start(v.at[high], obuf.at[i]) for i, v in enumerate(olds)]
    get += [copies.start(v.at[low], hbuf.at[i]) for i, v in enumerate(olds)]
    count_paths(1, mods, share, counts)
    for copy in get:
        copy.wait()
    put = [copies.start(hbuf.at[i], outs[i].at[low]) for i in range(4)]
    for i in range(2):
        add_paths(1, mods, share, cbuf.at[:, i], total)
        step_modules(total, counts, obuf.at[i], obuf.at[2 + i], nbuf.at[i], nbuf.at[2 + i])
        put.append(copies.start(nbuf.at[i], outs[i].at[high]))
        put.append(copies.start(nbuf.at[2 + i], outs[2 + i].at[high]))
    for copy in put:
        copy.wait()


def outer_second(sharing, came, weights, moments):
    whole = weights[0].shape
    mods = whole[0] // 2
    half = (mods,) + whole[1:]
    return pl.pallas_call(
        outer_second_kernel,
        out_shape=[jax.ShapeDtypeStruct(whole, bf16)] * 4,
        in_specs=[SMEM] + [HBM] * 5,
        out_specs=[HBM] * 4,
        scratch_shapes=[
            pltpu.VMEM(came.shape, bf16),
            pltpu.VMEM((4,) + half, bf16),
            pltpu.VMEM((4,) + half, bf16),
            pltpu.VMEM(half, f32),
            pltpu.VMEM((4,) + half, bf16),
            pltpu.SMEM((mods,), jnp.int32),
            pltpu.SemaphoreType.DMA((17,)),
        ],
        compiler_params=params(12),
        cost_estimate=cost(8 << 20, 8 << 20),
        name="outer_second",
    )(sharing, came, *weights, *moments)


def outer_first_kernel(share, came, *refs):
    olds, outs = refs[:4], refs[4:8]
    cbuf, obuf, total, nbuf, counts, sems = refs[8:]
    mods = counts.shape[0]
    low = pl.ds(0, mods)
    copies = Copies(sems)
    get = []
    for i in range(2):
        get.append([copies.start(came.at[:, i], cbuf.at[i])])
        get.append([copies.start(olds[j].at[low], obuf.at[j]) for j in (i, 2 + i)])
    count_paths(0, 0, share, counts)
    put = []
    for i in range(2):
        for copy in get[2 * i]:
            copy.wait()
        add_paths(0, 0, share, cbuf.at[i], total)
        for copy in get[2 * i + 1]:
            copy.wait()
        step_modules(total, counts, obuf.at[i], obuf.at[2 + i], nbuf.at[i], nbuf.at[2 + i])
        put.append(copies.start(nbuf.at[i], outs[i].at[low]))
        put.append(copies.start(nbuf.at[2 + i], outs[2 + i].at[low]))
    for copy in put:
        copy.wait()


def outer_first(sharing, came, before):
    whole = before[0].shape
    half = (whole[0] // 2,) + whole[1:]
    return pl.pallas_call(
        outer_first_kernel,
        out_shape=[jax.ShapeDtypeStruct(whole, bf16)] * 4,
        in_specs=[SMEM, HBM] + [HBM] * 4,
        out_specs=[HBM] * 4,
        input_output_aliases={2 + i: i for i in range(4)},
        scratch_shapes=[
            pltpu.VMEM((2, came.shape[0]) + came.shape[2:], bf16),
            pltpu.VMEM((4,) + half, bf16),
            pltpu.VMEM(half, f32),
            pltpu.VMEM((4,) + half, bf16),
            pltpu.SMEM(half[:1], jnp.int32),
            pltpu.SemaphoreType.DMA((10,)),
        ],
        compiler_params=params(12),
        cost_estimate=cost(8 << 20, 6 << 20),
        name="outer_first",
    )(sharing, came, *before)


def exchange(values):
    return lax.all_to_all(values, "path", split_axis=0, concat_axis=0, tiled=True)


def body(hidden_in, cotangent, up_weight, down_weight, up_moment, down_moment, sharing):
    depth = up_weight.shape[1] * lax.axis_size("path")
    width = up_weight.shape[2] * lax.axis_size("fsdp")
    chips = lax.axis_size("fsdp") // CORES
    scales = (1.0 / math.sqrt(depth), 1.0 / math.sqrt(width))
    tokens, cots = hidden_in[0], cotangent[0]
    sharing = jnp.transpose(sharing)
    weights, moments = (up_weight, down_weight), (up_moment, down_moment)

    came_first = exchange(pick(sharing, *weights, 0))
    tokens_wide = tokens.astype(f32)
    normed_first = gather_blocks((tokens_wide * row_scale(tokens_wide)).astype(bf16), chips)
    cots_all = gather_blocks(cots, chips)
    rows_second, normed_first, cots_all = lax.optimization_barrier(
        (pick(sharing, *weights, 1), normed_first, cots_all)
    )
    came_second = exchange(rows_second)

    own, send, hidden, slope = first_forward(normed_first, came_first, scales)
    middle, normed_own = middle_step(tokens, sum_blocks(own, send, chips))
    normed_second = settle(gather_blocks(normed_own, chips))

    own, send, grads_second = second_both(normed_second, cots_all, came_second, scales)
    back_second = exchange(grads_second)
    back_own = norm_back(cots, middle, sum_blocks(own, send, chips))
    back_middle = gather_blocks(back_own, chips)

    grads_first = first_back(back_middle, normed_first, came_first, hidden, slope, scales)
    back_first = exchange(grads_first)
    done = outer_second(sharing, back_second, weights, moments)
    new_up, new_down, new_up_moment, new_down_moment = outer_first(sharing, back_first, done)
    return (new_up, new_down, new_up_moment, new_down_moment)


def solution(mesh):
    tokens, pieces = P("path", "fsdp", None), P(None, "path", "fsdp")
    return jax.shard_map(
        body,
        mesh=mesh,
        in_specs=(tokens, tokens, pieces, pieces, pieces, pieces, P()),
        out_specs=(pieces,) * 4,
        check_vma=False,
    )
```

```python
import functools
import math

import jax
import jax.numpy as jnp
from jax import lax
from jax.experimental import pallas as pl
from jax.experimental.pallas import tpu as pltpu
from jax.sharding import PartitionSpec as P

inner_rate = 2.0
outer_rate = 0.7
keep_rate = 0.9
norm_eps = 1e-06
tanh_coeff = 0.7978845608028654
cube_coeff = 0.044715

f32 = jnp.float32
bf16 = jnp.bfloat16
HBM = pl.BlockSpec(memory_space=pl.ANY)
SMEM = pl.BlockSpec(memory_space=pltpu.SMEM)
VMEM = pl.BlockSpec(memory_space=pltpu.VMEM)
CORES = 2


def gelu_both(values):
    square = values * values
    tangent = jnp.tanh(tanh_coeff * (values + cube_coeff * values * square))
    half = 0.5 * (1.0 + tangent)
    slope = half + 0.5 * values * (1.0 - tangent * tangent) * tanh_coeff * (
        1.0 + 3.0 * cube_coeff * square
    )
    return (values * half, slope)


def row_scale(values):
    return lax.rsqrt(jnp.mean(values * values, axis=-1, keepdims=True) + norm_eps)


def nn(left, right):
    return jnp.dot(left, right, preferred_element_type=f32)


def nt(left, right):
    return lax.dot_general(left, right, (((1,), (1,)), ((), ())), preferred_element_type=f32)


def tn(left, right):
    return lax.dot_general(left, right, (((0,), (0,)), ((), ())), preferred_element_type=f32)


def params(mib):
    return pltpu.CompilerParams(vmem_limit_bytes=mib * 1024 * 1024)


def cost(flops, moved):
    return pl.CostEstimate(flops=flops, bytes_accessed=moved, transcendentals=0)


class Copies:
    def __init__(self, sems):
        self.sems, self.used = sems, 0

    def start(self, source, target):
        copy = pltpu.make_async_copy(source, target, self.sems.at[self.used])
        self.used += 1
        copy.start()
        return copy


def pick_kernel(level, share, up_w, down_w, out, buf, sems):
    paths = out.shape[0]
    copies = Copies(sems)
    got = []
    for p in range(paths):
        module = share[level, p]
        got.append(copies.start(up_w.at[module], buf.at[p, 0]))
        got.append(copies.start(down_w.at[module], buf.at[p, 1]))
    put = []
    for p in range(0, paths, 4):
        for copy in got[2 * p : 2 * p + 8]:
            copy.wait()
        some = pl.ds(p, 4)
        put.append(copies.start(buf.at[some], out.at[some]))
    for copy in put:
        copy.wait()


def pick(sharing, up_w, down_w, level):
    paths = sharing.shape[1]
    rows, cols = up_w.shape[1:]
    return pl.pallas_call(
        functools.partial(pick_kernel, level),
        out_shape=jax.ShapeDtypeStruct((paths, 2, rows, cols), bf16),
        in_specs=[SMEM, HBM, HBM],
        out_specs=HBM,
        scratch_shapes=[
            pltpu.VMEM((paths, 2, rows, cols), bf16),
            pltpu.SemaphoreType.DMA((2 * paths + paths // 4,)),
        ],
        compiler_params=params(60),
        cost_estimate=cost(0, 4 * paths * rows * cols * 2),
        name=f"pick_{level}",
    )(sharing, up_w, down_w)


def first_kernel(scales, *refs):
    in_scale, hid_scale = scales
    n = 8
    normed, came = refs[:n], refs[n]
    own, send, hidden, slope = refs[n + 1 : n + 5]
    nbuf, ubuf, wbuf, obuf, sbuf, hbuf, dbuf, sems = refs[n + 5 :]
    copies = Copies(sems)

    def fetch(i):
        return copies.start(normed[i], nbuf.at[i // 2, pl.ds((i % 2) * 128, 128)])

    get = [copies.start(came.at[:, 0], ubuf), fetch(0), fetch(1)]
    for copy in get:
        copy.wait()
    get_n = [fetch(i) for i in range(2, n)]
    get_w = copies.start(came.at[:, 1], wbuf)
    put = []
    for k in range(4):
        if k:
            get_n[2 * k - 2].wait()
            get_n[2 * k - 1].wait()
        value, back = gelu_both(nn(nbuf[k], ubuf[...].reshape(1024, 512)) * in_scale)
        hbuf[k] = value.astype(bf16)
        dbuf[k] = back.astype(bf16)
        put.append(copies.start(hbuf.at[k], hidden.at[k]))
        put.append(copies.start(dbuf.at[k], slope.at[k]))
    get_w.wait()
    for k in range(4):
        branch = nt(hbuf[k], wbuf[...].reshape(1024, 512)) * hid_scale
        obuf[k] = branch[:128].astype(bf16)
        sbuf[k] = branch[128:].astype(bf16)
        put.append(copies.start(sbuf.at[k], send.at[k]))
        put.append(copies.start(obuf.at[k], own.at[k]))
    for copy in put:
        copy.wait()


def first_forward(normed, came, scales):
    shapes = [((4, 128, 1024), bf16), ((4, 128, 1024), bf16), ((4, 256, 512), bf16), ((4, 256, 512), bf16)]
    return pl.pallas_call(
        functools.partial(first_kernel, scales),
        out_shape=[jax.ShapeDtypeStruct(*s) for s in shapes],
        in_specs=[HBM] * 9,
        out_specs=[HBM] * 4,
        scratch_shapes=[
            pltpu.VMEM((4, 256, 1024), bf16),
            pltpu.VMEM((32, 32, 512), bf16),
            pltpu.VMEM((32, 32, 512), bf16),
        ]
        + [pltpu.VMEM(*s) for s in shapes]
        + [pltpu.SemaphoreType.DMA((26,))],
        compiler_params=params(60),
        cost_estimate=cost(2 * 2 * 1024 * 1024 * 512, 10 << 20),
        name="first_forward",
    )(*normed, came)


def second_kernel(scales, *refs):
    in_scale, hid_scale = scales
    n = 8
    normed, cots, came = refs[:n], refs[n : 2 * n], refs[2 * n]
    own, send, grads = refs[2 * n + 1 : 2 * n + 4]
    nbuf, gbuf, ubuf, wbuf, obuf, sbuf, hbuf, pbuf, dbuf, outbuf, sems = refs[2 * n + 4 :]
    copies = Copies(sems)

    def fetch(sources, target, i):
        return copies.start(sources[i], target.at[pl.ds(i * 128, 128)])

    get = [copies.start(came.at[:, 0], ubuf), fetch(normed, nbuf, 0), fetch(normed, nbuf, 1)]
    get_n = [fetch(normed, nbuf, i) for i in range(2, n)]
    get_w = copies.start(came.at[:, 1], wbuf)
    get_g = [fetch(cots, gbuf, i) for i in range(n)]
    for copy in get:
        copy.wait()
    put = []
    blocks = [pl.ds(k * 256, 256) for k in range(4)]

    def product(k):
        return nn(nbuf[blocks[k]], ubuf[...].reshape(1024, 512)) * in_scale

    def activate(k, pre):
        value, slope = gelu_both(pre)
        hbuf[blocks[k]] = value.astype(bf16)
        dbuf[blocks[k]] = slope

    def back(k):
        return nn(gbuf[blocks[k]], wbuf[...].reshape(1024, 512)) * hid_scale

    def scaled(k, hidden):
        pbuf[blocks[k]] = (hidden * dbuf[blocks[k]]).astype(bf16)

    def normed_back(k):
        total = nt(pbuf[blocks[k]], ubuf[...].reshape(1024, 512)) * in_scale
        obuf[k] = total[:128].astype(bf16)
        sbuf[k] = total[128:].astype(bf16)
        put.append(copies.start(sbuf.at[k], send.at[k]))
        put.append(copies.start(obuf.at[k], own.at[k]))

    pre = product(0)
    for copy in get_n:
        copy.wait()
    for k in range(3):
        ahead = product(k + 1)
        activate(k, pre)
        pre = ahead
    get_w.wait()
    for copy in get_g:
        copy.wait()
    hidden = back(0)
    activate(3, pre)
    for k in range(3):
        ahead = back(k + 1)
        scaled(k, hidden)
        hidden = ahead
    scaled(3, hidden)
    for k in range(4):
        normed_back(k)
    for i in range(4):
        cols = pl.ds(i * 256, 256)
        some = pl.ds(i * 8, 8)
        grad = tn(gbuf[:, cols], hbuf[...]) * (inner_rate * hid_scale)
        outbuf[some, 1] = grad.astype(bf16).reshape(8, 32, 512)
        put.append(copies.start(outbuf.at[some, 1], grads.at[some, 1]))
    for i in range(4):
        cols = pl.ds(i * 256, 256)
        some = pl.ds(i * 8, 8)
        grad = tn(nbuf[:, cols], pbuf[...]) * (inner_rate * in_scale)
        outbuf[some, 0] = grad.astype(bf16).reshape(8, 32, 512)
        put.append(copies.start(outbuf.at[some, 0], grads.at[some, 0]))
    for copy in put:
        copy.wait()


def second_both(normed, cots, came, scales):
    shapes = [((4, 128, 1024), bf16), ((4, 128, 1024), bf16), ((32, 2, 32, 512), bf16)]
    return pl.pallas_call(
        functools.partial(second_kernel, scales),
        out_shape=[jax.ShapeDtypeStruct(*s) for s in shapes],
        in_specs=[HBM] * 17,
        out_specs=[HBM] * 3,
        scratch_shapes=[
            pltpu.VMEM((1024, 1024), bf16),
            pltpu.VMEM((1024, 1024), bf16),
            pltpu.VMEM((32, 32, 512), bf16),
            pltpu.VMEM((32, 32, 512), bf16),
            pltpu.VMEM(*shapes[0]),
            pltpu.VMEM(*shapes[1]),
            pltpu.VMEM((1024, 512), bf16),
            pltpu.VMEM((1024, 512), bf16),
            pltpu.VMEM((1024, 512), f32),
            pltpu.VMEM(*shapes[2]),
            pltpu.SemaphoreType.DMA((40,)),
        ],
        compiler_params=params(60),
        cost_estimate=cost(5 * 2 * 1024 * 1024 * 512, 11 << 20),
        name="second_both",
    )(*normed, *cots, came)


def back_kernel(scales, *refs):
    in_scale, hid_scale = scales
    n = 8
    backs, normed, came, hidden, slope = refs[:n], refs[n : 2 * n], refs[2 * n], refs[2 * n + 1], refs[2 * n + 2]
    grads = refs[2 * n + 3]
    bbuf, nbuf, wbuf, hbuf, dbuf, pbuf, outbuf, sems = refs[2 * n + 4 :]
    copies = Copies(sems)

    def fetch(sources, target, i):
        return copies.start(sources[i], target.at[pl.ds(i * 128, 128)])

    def fetch_slope(k):
        return copies.start(slope.at[k], dbuf.at[pl.ds(k * 256, 256)])

    get_w = copies.start(came.at[:, 1], wbuf)
    get = [[fetch(backs, bbuf, 2 * k), fetch(backs, bbuf, 2 * k + 1), fetch_slope(k)] for k in range(4)]
    get_h = copies.start(hidden, hbuf)
    get_n = [fetch(normed, nbuf, i) for i in range(n)]
    get_w.wait()
    for k in range(4):
        rows = pl.ds(k * 256, 256)
        for copy in get[k]:
            copy.wait()
        back_hidden = nn(bbuf[rows], wbuf[...].reshape(1024, 512)) * hid_scale
        pbuf[rows] = (back_hidden * dbuf[rows].astype(f32)).astype(bf16)
    get_h.wait()
    for copy in get_n:
        copy.wait()
    put = []
    for i in range(4):
        cols = pl.ds(i * 256, 256)
        some = pl.ds(i * 8, 8)
        grad = tn(bbuf[:, cols], hbuf[...].reshape(1024, 512)) * (inner_rate * hid_scale)
        outbuf[some, 1] = grad.astype(bf16).reshape(8, 32, 512)
        grad = tn(nbuf[:, cols], pbuf[...]) * (inner_rate * in_scale)
        outbuf[some, 0] = grad.astype(bf16).reshape(8, 32, 512)
        put.append(copies.start(outbuf.at[some], grads.at[some]))
    for copy in put:
        copy.wait()


def first_back(backs, normed, came, hidden, slope, scales):
    return pl.pallas_call(
        functools.partial(back_kernel, scales),
        out_shape=jax.ShapeDtypeStruct((32, 2, 32, 512), bf16),
        in_specs=[HBM] * 19,
        out_specs=HBM,
        scratch_shapes=[
            pltpu.VMEM((1024, 1024), bf16),
            pltpu.VMEM((1024, 1024), bf16),
            pltpu.VMEM((32, 32, 512), bf16),
            pltpu.VMEM((4, 256, 512), bf16),
            pltpu.VMEM((1024, 512), bf16),
            pltpu.VMEM((1024, 512), bf16),
            pltpu.VMEM((32, 2, 32, 512), bf16),
            pltpu.SemaphoreType.DMA((40,)),
        ],
        compiler_params=params(60),
        cost_estimate=cost(3 * 2 * 1024 * 1024 * 512, 10 << 20),
        name="first_back",
    )(*backs, *normed, came, hidden, slope)


def pair_kernel(own, got, first, *rest):
    first[...] = own[0].astype(f32) + got[0].astype(f32)
    for k in range(1, 4):
        rest[k - 1][...] = (own[k].astype(f32) + got[k].astype(f32)).astype(bf16)


def pair_sum(own, got):
    block = own.shape[1:]
    return pl.pallas_call(
        pair_kernel,
        out_shape=[jax.ShapeDtypeStruct(block, f32)] + [jax.ShapeDtypeStruct(block, bf16)] * 3,
        in_specs=[VMEM] * 2,
        out_specs=[VMEM] * 4,
        compiler_params=params(12),
        cost_estimate=cost(1 << 20, 5 << 20),
        name="pair_sum",
    )(own, got)


def middle_kernel(tokens, total, one, two, three, middle, normed):
    value = total[...] + one[...].astype(f32) + two[...].astype(f32) + three[...].astype(f32)
    value = value + tokens[...].astype(f32)
    middle[...] = value
    normed[...] = (value * row_scale(value)).astype(bf16)


def middle_step(tokens, parts):
    return pl.pallas_call(
        middle_kernel,
        out_shape=[jax.ShapeDtypeStruct(tokens.shape, f32), jax.ShapeDtypeStruct(tokens.shape, bf16)],
        in_specs=[VMEM] * 5,
        out_specs=[VMEM] * 2,
        compiler_params=params(12),
        cost_estimate=cost(1 << 20, 2 << 20),
        name="middle_step",
    )(tokens, *parts)


def norm_back_kernel(cots, middle, total, one, two, three, out):
    back = total[...] + one[...].astype(f32) + two[...].astype(f32) + three[...].astype(f32)
    scale = row_scale(middle[...])
    unit = middle[...] * scale
    centred = back - unit * jnp.mean(back * unit, axis=-1, keepdims=True)
    out[...] = (cots[...].astype(f32) + scale * centred).astype(bf16)


def norm_back(cots, middle, parts):
    return pl.pallas_call(
        norm_back_kernel,
        out_shape=jax.ShapeDtypeStruct(cots.shape, bf16),
        in_specs=[VMEM] * 6,
        out_specs=VMEM,
        compiler_params=params(12),
        cost_estimate=cost(1 << 20, 3 << 20),
        name="norm_back",
    )(cots, middle, *parts)


def chip_shift(by, chips):
    return [(y * CORES + c, ((y + by) % chips) * CORES + c) for y in range(chips) for c in range(CORES)]


def by_distance(chips):
    return sorted(range(1, chips), key=lambda k: -min(k, chips - k))


def other_core(chips):
    return [(i, i ^ 1) for i in range(chips * CORES)]


def gather_blocks(own, chips):
    held = {0: own}
    for k in by_distance(chips):
        held[k] = lax.ppermute(own, "fsdp", chip_shift(-k, chips))
    other = {k: lax.ppermute(v, "fsdp", other_core(chips)) for k, v in held.items()}
    return [v for k in range(chips) for v in (held[k], other[k])]


def settle_kernel(*refs):
    pass


def settle(values):
    count = len(values)
    return pl.pallas_call(
        settle_kernel,
        out_shape=[jax.ShapeDtypeStruct(v.shape, v.dtype) for v in values],
        in_specs=[HBM] * count,
        out_specs=[HBM] * count,
        input_output_aliases={i: i for i in range(count)},
        compiler_params=params(60),
        cost_estimate=cost(0, 4 << 20),
        name="settle",
    )(*values)


def sum_blocks(own, send, chips):
    got = lax.ppermute(send, "fsdp", other_core(chips))
    parts = pair_sum(own, got)
    return [parts[0]] + [lax.ppermute(parts[k], "fsdp", chip_shift(k, chips)) for k in by_distance(chips)]


def add_paths(level, low, share, came, total):
    def add(p, carry):
        m = share[level, p] - low
        total[m] += came[p].astype(f32)
        return carry

    total[...] = jnp.zeros_like(total)
    lax.fori_loop(0, came.shape[0], add, 0, unroll=4)


def step_modules(total, counts, old_weight, old_moment, wout, mout):
    def step(m, carry):
        mean = total[m] / counts[m].astype(f32)
        moment = keep_rate * old_moment[m].astype(f32) + mean
        weight = old_weight[m].astype(f32) - outer_rate * (mean + keep_rate * moment)
        wout[m] = weight.astype(bf16)
        mout[m] = moment.astype(bf16)
        return carry

    lax.fori_loop(0, wout.shape[0], step, 0, unroll=2)


def count_paths(level, low, share, counts):
    for m in range(counts.shape[0]):
        counts[m] = 0
    for p in range(share.shape[1]):
        m = share[level, p] - low
        counts[m] = counts[m] + 1


def outer_second_kernel(share, came, up_w, down_w, up_m, down_m, *refs):
    outs = refs[:4]
    cbuf, obuf, hbuf, total, nbuf, counts, sems = refs[4:]
    mods = counts.shape[0]
    low, high = pl.ds(0, mods), pl.ds(mods, mods)
    copies = Copies(sems)
    olds = (up_w, down_w, up_m, down_m)
    get = [copies.start(came, cbuf)] + [copies.start(v.at[high], obuf.at[i]) for i, v in enumerate(olds)]
    get += [copies.start(v.at[low], hbuf.at[i]) for i, v in enumerate(olds)]
    count_paths(1, mods, share, counts)
    for copy in get:
        copy.wait()
    put = [copies.start(hbuf.at[i], outs[i].at[low]) for i in range(4)]
    for i in range(2):
        add_paths(1, mods, share, cbuf.at[:, i], total)
        step_modules(total, counts, obuf.at[i], obuf.at[2 + i], nbuf.at[i], nbuf.at[2 + i])
        put.append(copies.start(nbuf.at[i], outs[i].at[high]))
        put.append(copies.start(nbuf.at[2 + i], outs[2 + i].at[high]))
    for copy in put:
        copy.wait()


def outer_second(sharing, came, weights, moments):
    whole = weights[0].shape
    mods = whole[0] // 2
    half = (mods,) + whole[1:]
    return pl.pallas_call(
        outer_second_kernel,
        out_shape=[jax.ShapeDtypeStruct(whole, bf16)] * 4,
        in_specs=[SMEM] + [HBM] * 5,
        out_specs=[HBM] * 4,
        scratch_shapes=[
            pltpu.VMEM(came.shape, bf16),
            pltpu.VMEM((4,) + half, bf16),
            pltpu.VMEM((4,) + half, bf16),
            pltpu.VMEM(half, f32),
            pltpu.VMEM((4,) + half, bf16),
            pltpu.SMEM((mods,), jnp.int32),
            pltpu.SemaphoreType.DMA((17,)),
        ],
        compiler_params=params(12),
        cost_estimate=cost(8 << 20, 8 << 20),
        name="outer_second",
    )(sharing, came, *weights, *moments)


def outer_first_kernel(share, came, *refs):
    olds, outs = refs[:4], refs[4:8]
    cbuf, obuf, total, nbuf, counts, sems = refs[8:]
    mods = counts.shape[0]
    low = pl.ds(0, mods)
    copies = Copies(sems)
    get = []
    for i in range(2):
        get.append([copies.start(came.at[:, i], cbuf.at[i])])
        get.append([copies.start(olds[j].at[low], obuf.at[j]) for j in (i, 2 + i)])
    count_paths(0, 0, share, counts)
    put = []
    for i in range(2):
        for copy in get[2 * i]:
            copy.wait()
        add_paths(0, 0, share, cbuf.at[i], total)
        for copy in get[2 * i + 1]:
            copy.wait()
        step_modules(total, counts, obuf.at[i], obuf.at[2 + i], nbuf.at[i], nbuf.at[2 + i])
        put.append(copies.start(nbuf.at[i], outs[i].at[low]))
        put.append(copies.start(nbuf.at[2 + i], outs[2 + i].at[low]))
    for copy in put:
        copy.wait()


def outer_first(sharing, came, before):
    whole = before[0].shape
    half = (whole[0] // 2,) + whole[1:]
    return pl.pallas_call(
        outer_first_kernel,
        out_shape=[jax.ShapeDtypeStruct(whole, bf16)] * 4,
        in_specs=[SMEM, HBM] + [HBM] * 4,
        out_specs=[HBM] * 4,
        input_output_aliases={2 + i: i for i in range(4)},
        scratch_shapes=[
            pltpu.VMEM((2, came.shape[0]) + came.shape[2:], bf16),
            pltpu.VMEM((4,) + half, bf16),
            pltpu.VMEM(half, f32),
            pltpu.VMEM((4,) + half, bf16),
            pltpu.SMEM(half[:1], jnp.int32),
            pltpu.SemaphoreType.DMA((10,)),
        ],
        compiler_params=params(12),
        cost_estimate=cost(8 << 20, 6 << 20),
        name="outer_first",
    )(sharing, came, *before)


def exchange(values):
    return lax.all_to_all(values, "path", split_axis=0, concat_axis=0, tiled=True)


def body(hidden_in, cotangent, up_weight, down_weight, up_moment, down_moment, sharing):
    depth = up_weight.shape[1] * lax.axis_size("path")
    width = up_weight.shape[2] * lax.axis_size("fsdp")
    chips = lax.axis_size("fsdp") // CORES
    scales = (1.0 / math.sqrt(depth), 1.0 / math.sqrt(width))
    tokens, cots = hidden_in[0], cotangent[0]
    sharing = jnp.transpose(sharing)
    weights, moments = (up_weight, down_weight), (up_moment, down_moment)

    came_first = exchange(pick(sharing, *weights, 0))
    tokens_wide = tokens.astype(f32)
    normed_first = gather_blocks((tokens_wide * row_scale(tokens_wide)).astype(bf16), chips)
    cots_all = gather_blocks(cots, chips)
    rows_second, normed_first, cots_all = lax.optimization_barrier(
        (pick(sharing, *weights, 1), normed_first, cots_all)
    )
    came_second = exchange(rows_second)

    own, send, hidden, slope = first_forward(normed_first, came_first, scales)
    middle, normed_own = middle_step(tokens, sum_blocks(own, send, chips))
    normed_second = settle(gather_blocks(normed_own, chips))

    own, send, grads_second = second_both(normed_second, cots_all, came_second, scales)
    back_second = exchange(grads_second)
    back_own = norm_back(cots, middle, sum_blocks(own, send, chips))
    back_middle = gather_blocks(back_own, chips)

    grads_first = first_back(back_middle, normed_first, came_first, hidden, slope, scales)
    back_first = exchange(grads_first)
    done = outer_second(sharing, back_second, weights, moments)
    new_up, new_down, new_up_moment, new_down_moment = outer_first(sharing, back_first, done)
    return (new_up, new_down, new_up_moment, new_down_moment)


def solution(mesh):
    tokens, pieces = P("path", "fsdp", None), P(None, "path", "fsdp")
    return jax.shard_map(
        body,
        mesh=mesh,
        in_specs=(tokens, tokens, pieces, pieces, pieces, pieces, P()),
        out_specs=(pieces,) * 4,
        check_vma=False,
    )
```

```python
import functools
import math

import jax
import jax.numpy as jnp
from jax import lax
from jax.experimental import pallas as pl
from jax.experimental.pallas import tpu as pltpu
from jax.sharding import PartitionSpec as P

inner_rate = 2.0
outer_rate = 0.7
keep_rate = 0.9
norm_eps = 1e-06
tanh_coeff = 0.7978845608028654
cube_coeff = 0.044715

f32 = jnp.float32
bf16 = jnp.bfloat16
HBM = pl.BlockSpec(memory_space=pl.ANY)
SMEM = pl.BlockSpec(memory_space=pltpu.SMEM)
VMEM = pl.BlockSpec(memory_space=pltpu.VMEM)
CORES = 2


def gelu_both(values):
    square = values * values
    tangent = jnp.tanh(tanh_coeff * (values + cube_coeff * values * square))
    half = 0.5 * (1.0 + tangent)
    slope = half + 0.5 * values * (1.0 - tangent * tangent) * tanh_coeff * (
        1.0 + 3.0 * cube_coeff * square
    )
    return (values * half, slope)


def row_scale(values):
    return lax.rsqrt(jnp.mean(values * values, axis=-1, keepdims=True) + norm_eps)


def nn(left, right):
    return jnp.dot(left, right, preferred_element_type=f32)


def nt(left, right):
    return lax.dot_general(left, right, (((1,), (1,)), ((), ())), preferred_element_type=f32)


def tn(left, right):
    return lax.dot_general(left, right, (((0,), (0,)), ((), ())), preferred_element_type=f32)


def params(mib):
    return pltpu.CompilerParams(vmem_limit_bytes=mib * 1024 * 1024)


def cost(flops, moved):
    return pl.CostEstimate(flops=flops, bytes_accessed=moved, transcendentals=0)


class Copies:
    def __init__(self, sems):
        self.sems, self.used = sems, 0

    def start(self, source, target):
        copy = pltpu.make_async_copy(source, target, self.sems.at[self.used])
        self.used += 1
        copy.start()
        return copy


def pick_kernel(level, share, up_w, down_w, out, buf, sems):
    paths = out.shape[0]
    copies = Copies(sems)
    got = []
    for p in range(paths):
        module = share[level, p]
        got.append(copies.start(up_w.at[module], buf.at[p, 0]))
        got.append(copies.start(down_w.at[module], buf.at[p, 1]))
    put = []
    for p in range(0, paths, 4):
        for copy in got[2 * p : 2 * p + 8]:
            copy.wait()
        some = pl.ds(p, 4)
        put.append(copies.start(buf.at[some], out.at[some]))
    for copy in put:
        copy.wait()


def pick(sharing, up_w, down_w, level):
    paths = sharing.shape[1]
    rows, cols = up_w.shape[1:]
    return pl.pallas_call(
        functools.partial(pick_kernel, level),
        out_shape=jax.ShapeDtypeStruct((paths, 2, rows, cols), bf16),
        in_specs=[SMEM, HBM, HBM],
        out_specs=HBM,
        scratch_shapes=[
            pltpu.VMEM((paths, 2, rows, cols), bf16),
            pltpu.SemaphoreType.DMA((2 * paths + paths // 4,)),
        ],
        compiler_params=params(60),
        cost_estimate=cost(0, 4 * paths * rows * cols * 2),
        name=f"pick_{level}",
    )(sharing, up_w, down_w)


def first_kernel(scales, *refs):
    in_scale, hid_scale = scales
    n = 8
    normed, came = refs[:n], refs[n]
    own, send, hidden, slope = refs[n + 1 : n + 5]
    nbuf, ubuf, wbuf, obuf, sbuf, hbuf, dbuf, sems = refs[n + 5 :]
    copies = Copies(sems)

    def fetch(i):
        return copies.start(normed[i], nbuf.at[i // 2, pl.ds((i % 2) * 128, 128)])

    get = [copies.start(came.at[:, 0], ubuf), copies.start(came.at[:, 1], wbuf)]
    get += [fetch(i) for i in range(n)]
    for copy in get:
        copy.wait()
    put = []
    for k in range(4):
        value, back = gelu_both(nn(nbuf[k], ubuf[...].reshape(1024, 512)) * in_scale)
        hbuf[k] = value.astype(bf16)
        dbuf[k] = back.astype(bf16)
        put.append(copies.start(hbuf.at[k], hidden.at[k]))
        put.append(copies.start(dbuf.at[k], slope.at[k]))
    for k in range(4):
        branch = nt(hbuf[k], wbuf[...].reshape(1024, 512)) * hid_scale
        obuf[k] = branch[:128].astype(bf16)
        sbuf[k] = branch[128:].astype(bf16)
        put.append(copies.start(sbuf.at[k], send.at[k]))
        put.append(copies.start(obuf.at[k], own.at[k]))
    for copy in put:
        copy.wait()


def first_forward(normed, came, scales):
    shapes = [((4, 128, 1024), bf16), ((4, 128, 1024), bf16), ((4, 256, 512), bf16), ((4, 256, 512), bf16)]
    return pl.pallas_call(
        functools.partial(first_kernel, scales),
        out_shape=[jax.ShapeDtypeStruct(*s) for s in shapes],
        in_specs=[HBM] * 9,
        out_specs=[HBM] * 4,
        scratch_shapes=[
            pltpu.VMEM((4, 256, 1024), bf16),
            pltpu.VMEM((32, 32, 512), bf16),
            pltpu.VMEM((32, 32, 512), bf16),
        ]
        + [pltpu.VMEM(*s) for s in shapes]
        + [pltpu.SemaphoreType.DMA((26,))],
        compiler_params=params(60),
        cost_estimate=cost(2 * 2 * 1024 * 1024 * 512, 10 << 20),
        name="first_forward",
    )(*normed, came)


def second_kernel(scales, *refs):
    in_scale, hid_scale = scales
    n = 8
    normed, cots, came = refs[:n], refs[n : 2 * n], refs[2 * n]
    own, send, grads = refs[2 * n + 1 : 2 * n + 4]
    nbuf, gbuf, ubuf, wbuf, obuf, sbuf, hbuf, pbuf, dbuf, outbuf, sems = refs[2 * n + 4 :]
    copies = Copies(sems)

    def fetch(sources, target, i):
        return copies.start(sources[i], target.at[pl.ds(i * 128, 128)])

    get = [copies.start(came.at[:, 0], ubuf), fetch(normed, nbuf, 0), fetch(normed, nbuf, 1)]
    get_n = [fetch(normed, nbuf, i) for i in range(2, n)]
    get_w = copies.start(came.at[:, 1], wbuf)
    get_g = [fetch(cots, gbuf, i) for i in range(n)]
    for copy in get + get_n + [get_w] + get_g:
        copy.wait()
    put = []
    blocks = [pl.ds(k * 256, 256) for k in range(4)]

    def product(k):
        return nn(nbuf[blocks[k]], ubuf[...].reshape(1024, 512)) * in_scale

    def activate(k, pre):
        value, slope = gelu_both(pre)
        hbuf[blocks[k]] = value.astype(bf16)
        dbuf[blocks[k]] = slope

    def back(k):
        return nn(gbuf[blocks[k]], wbuf[...].reshape(1024, 512)) * hid_scale

    def scaled(k, hidden):
        pbuf[blocks[k]] = (hidden * dbuf[blocks[k]]).astype(bf16)

    def normed_back(k):
        total = nt(pbuf[blocks[k]], ubuf[...].reshape(1024, 512)) * in_scale
        obuf[k] = total[:128].astype(bf16)
        sbuf[k] = total[128:].astype(bf16)
        put.append(copies.start(sbuf.at[k], send.at[k]))
        put.append(copies.start(obuf.at[k], own.at[k]))

    pre = product(0)
    for k in range(3):
        ahead = product(k + 1)
        activate(k, pre)
        pre = ahead
    hidden = back(0)
    activate(3, pre)
    for k in range(3):
        ahead = back(k + 1)
        scaled(k, hidden)
        hidden = ahead
    scaled(3, hidden)
    for k in range(4):
        normed_back(k)
    for i in range(4):
        cols = pl.ds(i * 256, 256)
        some = pl.ds(i * 8, 8)
        grad = tn(gbuf[:, cols], hbuf[...]) * (inner_rate * hid_scale)
        outbuf[some, 1] = grad.astype(bf16).reshape(8, 32, 512)
        put.append(copies.start(outbuf.at[some, 1], grads.at[some, 1]))
    for i in range(4):
        cols = pl.ds(i * 256, 256)
        some = pl.ds(i * 8, 8)
        grad = tn(nbuf[:, cols], pbuf[...]) * (inner_rate * in_scale)
        outbuf[some, 0] = grad.astype(bf16).reshape(8, 32, 512)
        put.append(copies.start(outbuf.at[some, 0], grads.at[some, 0]))
    for copy in put:
        copy.wait()


def second_both(normed, cots, came, scales):
    shapes = [((4, 128, 1024), bf16), ((4, 128, 1024), bf16), ((32, 2, 32, 512), bf16)]
    return pl.pallas_call(
        functools.partial(second_kernel, scales),
        out_shape=[jax.ShapeDtypeStruct(*s) for s in shapes],
        in_specs=[HBM] * 17,
        out_specs=[HBM] * 3,
        scratch_shapes=[
            pltpu.VMEM((1024, 1024), bf16),
            pltpu.VMEM((1024, 1024), bf16),
            pltpu.VMEM((32, 32, 512), bf16),
            pltpu.VMEM((32, 32, 512), bf16),
            pltpu.VMEM(*shapes[0]),
            pltpu.VMEM(*shapes[1]),
            pltpu.VMEM((1024, 512), bf16),
            pltpu.VMEM((1024, 512), bf16),
            pltpu.VMEM((1024, 512), f32),
            pltpu.VMEM(*shapes[2]),
            pltpu.SemaphoreType.DMA((40,)),
        ],
        compiler_params=params(60),
        cost_estimate=cost(5 * 2 * 1024 * 1024 * 512, 11 << 20),
        name="second_both",
    )(*normed, *cots, came)


def back_kernel(scales, *refs):
    in_scale, hid_scale = scales
    n = 8
    backs, normed, came, hidden, slope = refs[:n], refs[n : 2 * n], refs[2 * n], refs[2 * n + 1], refs[2 * n + 2]
    grads = refs[2 * n + 3]
    bbuf, nbuf, wbuf, hbuf, dbuf, pbuf, outbuf, sems = refs[2 * n + 4 :]
    copies = Copies(sems)

    def fetch(sources, target, i):
        return copies.start(sources[i], target.at[pl.ds(i * 128, 128)])

    def fetch_slope(k):
        return copies.start(slope.at[k], dbuf.at[pl.ds(k * 256, 256)])

    get_w = copies.start(came.at[:, 1], wbuf)
    get = [[fetch(backs, bbuf, 2 * k), fetch(backs, bbuf, 2 * k + 1), fetch_slope(k)] for k in range(4)]
    get_h = copies.start(hidden, hbuf)
    get_n = [fetch(normed, nbuf, i) for i in range(n)]
    get_w.wait()
    for k in range(4):
        rows = pl.ds(k * 256, 256)
        for copy in get[k]:
            copy.wait()
        back_hidden = nn(bbuf[rows], wbuf[...].reshape(1024, 512)) * hid_scale
        pbuf[rows] = (back_hidden * dbuf[rows].astype(f32)).astype(bf16)
    get_h.wait()
    for copy in get_n:
        copy.wait()
    put = []
    for i in range(4):
        cols = pl.ds(i * 256, 256)
        some = pl.ds(i * 8, 8)
        grad = tn(bbuf[:, cols], hbuf[...].reshape(1024, 512)) * (inner_rate * hid_scale)
        outbuf[some, 1] = grad.astype(bf16).reshape(8, 32, 512)
        grad = tn(nbuf[:, cols], pbuf[...]) * (inner_rate * in_scale)
        outbuf[some, 0] = grad.astype(bf16).reshape(8, 32, 512)
        put.append(copies.start(outbuf.at[some], grads.at[some]))
    for copy in put:
        copy.wait()


def first_back(backs, normed, came, hidden, slope, scales):
    return pl.pallas_call(
        functools.partial(back_kernel, scales),
        out_shape=jax.ShapeDtypeStruct((32, 2, 32, 512), bf16),
        in_specs=[HBM] * 19,
        out_specs=HBM,
        scratch_shapes=[
            pltpu.VMEM((1024, 1024), bf16),
            pltpu.VMEM((1024, 1024), bf16),
            pltpu.VMEM((32, 32, 512), bf16),
            pltpu.VMEM((4, 256, 512), bf16),
            pltpu.VMEM((1024, 512), bf16),
            pltpu.VMEM((1024, 512), bf16),
            pltpu.VMEM((32, 2, 32, 512), bf16),
            pltpu.SemaphoreType.DMA((40,)),
        ],
        compiler_params=params(60),
        cost_estimate=cost(3 * 2 * 1024 * 1024 * 512, 10 << 20),
        name="first_back",
    )(*backs, *normed, came, hidden, slope)


def pair_kernel(own, got, first, *rest):
    first[...] = own[0].astype(f32) + got[0].astype(f32)
    for k in range(1, 4):
        rest[k - 1][...] = (own[k].astype(f32) + got[k].astype(f32)).astype(bf16)


def pair_sum(own, got):
    block = own.shape[1:]
    return pl.pallas_call(
        pair_kernel,
        out_shape=[jax.ShapeDtypeStruct(block, f32)] + [jax.ShapeDtypeStruct(block, bf16)] * 3,
        in_specs=[VMEM] * 2,
        out_specs=[VMEM] * 4,
        compiler_params=params(12),
        cost_estimate=cost(1 << 20, 5 << 20),
        name="pair_sum",
    )(own, got)


def middle_kernel(tokens, total, one, two, three, middle, normed):
    value = total[...] + one[...].astype(f32) + two[...].astype(f32) + three[...].astype(f32)
    value = value + tokens[...].astype(f32)
    middle[...] = value
    normed[...] = (value * row_scale(value)).astype(bf16)


def middle_step(tokens, parts):
    return pl.pallas_call(
        middle_kernel,
        out_shape=[jax.ShapeDtypeStruct(tokens.shape, f32), jax.ShapeDtypeStruct(tokens.shape, bf16)],
        in_specs=[VMEM] * 5,
        out_specs=[VMEM] * 2,
        compiler_params=params(12),
        cost_estimate=cost(1 << 20, 2 << 20),
        name="middle_step",
    )(tokens, *parts)


def norm_back_kernel(cots, middle, total, one, two, three, out):
    back = total[...] + one[...].astype(f32) + two[...].astype(f32) + three[...].astype(f32)
    scale = row_scale(middle[...])
    unit = middle[...] * scale
    centred = back - unit * jnp.mean(back * unit, axis=-1, keepdims=True)
    out[...] = (cots[...].astype(f32) + scale * centred).astype(bf16)


def norm_back(cots, middle, parts):
    return pl.pallas_call(
        norm_back_kernel,
        out_shape=jax.ShapeDtypeStruct(cots.shape, bf16),
        in_specs=[VMEM] * 6,
        out_specs=VMEM,
        compiler_params=params(12),
        cost_estimate=cost(1 << 20, 3 << 20),
        name="norm_back",
    )(cots, middle, *parts)


def chip_shift(by, chips):
    return [(y * CORES + c, ((y + by) % chips) * CORES + c) for y in range(chips) for c in range(CORES)]


def by_distance(chips):
    return sorted(range(1, chips), key=lambda k: -min(k, chips - k))


def other_core(chips):
    return [(i, i ^ 1) for i in range(chips * CORES)]


def gather_blocks(own, chips):
    held = {0: own}
    for k in by_distance(chips):
        held[k] = lax.ppermute(own, "fsdp", chip_shift(-k, chips))
    other = {k: lax.ppermute(v, "fsdp", other_core(chips)) for k, v in held.items()}
    return [v for k in range(chips) for v in (held[k], other[k])]


def settle_kernel(*refs):
    pass


def settle(values):
    count = len(values)
    return pl.pallas_call(
        settle_kernel,
        out_shape=[jax.ShapeDtypeStruct(v.shape, v.dtype) for v in values],
        in_specs=[HBM] * count,
        out_specs=[HBM] * count,
        input_output_aliases={i: i for i in range(count)},
        compiler_params=params(60),
        cost_estimate=cost(0, 4 << 20),
        name="settle",
    )(*values)


def sum_blocks(own, send, chips):
    got = lax.ppermute(send, "fsdp", other_core(chips))
    parts = pair_sum(own, got)
    return [parts[0]] + [lax.ppermute(parts[k], "fsdp", chip_shift(k, chips)) for k in by_distance(chips)]


def add_paths(level, low, share, came, total):
    def add(p, carry):
        m = share[level, p] - low
        total[m] += came[p].astype(f32)
        return carry

    total[...] = jnp.zeros_like(total)
    lax.fori_loop(0, came.shape[0], add, 0, unroll=4)


def step_modules(total, counts, old_weight, old_moment, wout, mout):
    def step(m, carry):
        mean = total[m] / counts[m].astype(f32)
        moment = keep_rate * old_moment[m].astype(f32) + mean
        weight = old_weight[m].astype(f32) - outer_rate * (mean + keep_rate * moment)
        wout[m] = weight.astype(bf16)
        mout[m] = moment.astype(bf16)
        return carry

    lax.fori_loop(0, wout.shape[0], step, 0, unroll=2)


def count_paths(level, low, share, counts):
    for m in range(counts.shape[0]):
        counts[m] = 0
    for p in range(share.shape[1]):
        m = share[level, p] - low
        counts[m] = counts[m] + 1


def outer_second_kernel(share, came, up_w, down_w, up_m, down_m, *refs):
    outs = refs[:4]
    cbuf, obuf, hbuf, total, nbuf, counts, sems = refs[4:]
    mods = counts.shape[0]
    low, high = pl.ds(0, mods), pl.ds(mods, mods)
    copies = Copies(sems)
    olds = (up_w, down_w, up_m, down_m)
    get = [copies.start(came, cbuf)] + [copies.start(v.at[high], obuf.at[i]) for i, v in enumerate(olds)]
    get += [copies.start(v.at[low], hbuf.at[i]) for i, v in enumerate(olds)]
    count_paths(1, mods, share, counts)
    for copy in get:
        copy.wait()
    put = [copies.start(hbuf.at[i], outs[i].at[low]) for i in range(4)]
    for i in range(2):
        add_paths(1, mods, share, cbuf.at[:, i], total)
        step_modules(total, counts, obuf.at[i], obuf.at[2 + i], nbuf.at[i], nbuf.at[2 + i])
        put.append(copies.start(nbuf.at[i], outs[i].at[high]))
        put.append(copies.start(nbuf.at[2 + i], outs[2 + i].at[high]))
    for copy in put:
        copy.wait()


def outer_second(sharing, came, weights, moments):
    whole = weights[0].shape
    mods = whole[0] // 2
    half = (mods,) + whole[1:]
    return pl.pallas_call(
        outer_second_kernel,
        out_shape=[jax.ShapeDtypeStruct(whole, bf16)] * 4,
        in_specs=[SMEM] + [HBM] * 5,
        out_specs=[HBM] * 4,
        scratch_shapes=[
            pltpu.VMEM(came.shape, bf16),
            pltpu.VMEM((4,) + half, bf16),
            pltpu.VMEM((4,) + half, bf16),
            pltpu.VMEM(half, f32),
            pltpu.VMEM((4,) + half, bf16),
            pltpu.SMEM((mods,), jnp.int32),
            pltpu.SemaphoreType.DMA((17,)),
        ],
        compiler_params=params(12),
        cost_estimate=cost(8 << 20, 8 << 20),
        name="outer_second",
    )(sharing, came, *weights, *moments)


def outer_first_kernel(share, came, *refs):
    olds, outs = refs[:4], refs[4:8]
    cbuf, obuf, total, nbuf, counts, sems = refs[8:]
    mods = counts.shape[0]
    low = pl.ds(0, mods)
    copies = Copies(sems)
    get = []
    for i in range(2):
        get.append([copies.start(came.at[:, i], cbuf.at[i])])
        get.append([copies.start(olds[j].at[low], obuf.at[j]) for j in (i, 2 + i)])
    count_paths(0, 0, share, counts)
    put = []
    for i in range(2):
        for copy in get[2 * i]:
            copy.wait()
        add_paths(0, 0, share, cbuf.at[i], total)
        for copy in get[2 * i + 1]:
            copy.wait()
        step_modules(total, counts, obuf.at[i], obuf.at[2 + i], nbuf.at[i], nbuf.at[2 + i])
        put.append(copies.start(nbuf.at[i], outs[i].at[low]))
        put.append(copies.start(nbuf.at[2 + i], outs[2 + i].at[low]))
    for copy in put:
        copy.wait()


def outer_first(sharing, came, before):
    whole = before[0].shape
    half = (whole[0] // 2,) + whole[1:]
    return pl.pallas_call(
        outer_first_kernel,
        out_shape=[jax.ShapeDtypeStruct(whole, bf16)] * 4,
        in_specs=[SMEM, HBM] + [HBM] * 4,
        out_specs=[HBM] * 4,
        input_output_aliases={2 + i: i for i in range(4)},
        scratch_shapes=[
            pltpu.VMEM((2, came.shape[0]) + came.shape[2:], bf16),
            pltpu.VMEM((4,) + half, bf16),
            pltpu.VMEM(half, f32),
            pltpu.VMEM((4,) + half, bf16),
            pltpu.SMEM(half[:1], jnp.int32),
            pltpu.SemaphoreType.DMA((10,)),
        ],
        compiler_params=params(12),
        cost_estimate=cost(8 << 20, 6 << 20),
        name="outer_first",
    )(sharing, came, *before)


def exchange(values):
    return lax.all_to_all(values, "path", split_axis=0, concat_axis=0, tiled=True)


def body(hidden_in, cotangent, up_weight, down_weight, up_moment, down_moment, sharing):
    depth = up_weight.shape[1] * lax.axis_size("path")
    width = up_weight.shape[2] * lax.axis_size("fsdp")
    chips = lax.axis_size("fsdp") // CORES
    scales = (1.0 / math.sqrt(depth), 1.0 / math.sqrt(width))
    tokens, cots = hidden_in[0], cotangent[0]
    sharing = jnp.transpose(sharing)
    weights, moments = (up_weight, down_weight), (up_moment, down_moment)

    came_first = exchange(pick(sharing, *weights, 0))
    tokens_wide = tokens.astype(f32)
    normed_first = gather_blocks((tokens_wide * row_scale(tokens_wide)).astype(bf16), chips)
    cots_all = gather_blocks(cots, chips)
    rows_second, normed_first, cots_all = lax.optimization_barrier(
        (pick(sharing, *weights, 1), normed_first, cots_all)
    )
    came_second = exchange(rows_second)

    own, send, hidden, slope = first_forward(normed_first, came_first, scales)
    middle, normed_own = middle_step(tokens, sum_blocks(own, send, chips))
    normed_second = settle(gather_blocks(normed_own, chips))

    own, send, grads_second = second_both(normed_second, cots_all, came_second, scales)
    back_second = exchange(grads_second)
    back_own = norm_back(cots, middle, sum_blocks(own, send, chips))
    back_middle = gather_blocks(back_own, chips)

    grads_first = first_back(back_middle, normed_first, came_first, hidden, slope, scales)
    back_first = exchange(grads_first)
    done = outer_second(sharing, back_second, weights, moments)
    new_up, new_down, new_up_moment, new_down_moment = outer_first(sharing, back_first, done)
    return (new_up, new_down, new_up_moment, new_down_moment)


def solution(mesh):
    tokens, pieces = P("path", "fsdp", None), P(None, "path", "fsdp")
    return jax.shard_map(
        body,
        mesh=mesh,
        in_specs=(tokens, tokens, pieces, pieces, pieces, pieces, P()),
        out_specs=(pieces,) * 4,
        check_vma=False,
    )
```
